128 devices in a mesh: row: 16 (over x, z_hi, core), col: 8 (over z_lo, y).
Axes of the slice: x: 4, y: 4, z: 4 (z_hi: 2, z_lo: 2; z = z_hi * 2 + z_lo), core: 2. Of those that a mesh axis runs over, the one named last changes fastest.
Arguments:
- pair: bfloat16 [1024, 1024, 128], P(('row', 'col')), may hold values from -6 to 6
- norm_gain: float32 [2, 128], replicated, may hold values from 0.25 to 1.75
- proj_weight: bfloat16 [2, 128, 512], replicated, may hold values from -8 to 8
- out_weight: bfloat16 [2, 128, 128], replicated, may hold values from -1 to 1
- bias_weight: bfloat16 [2, 128, 4], replicated, may hold values from -7 to 7
Outputs:
- updated: bfloat16 [1024, 1024, 128], P(('row', 'col'))
The draws below stay inside these ranges and needn't reach their ends.
All inputs are finite; a program needn't handle non-finite values.
Results may differ from the reference program's by a relative error of at most 0.025.
Values may be sent and summed in bfloat16 or wider, within the bound.
No kernel may reach another device: no remote copies, remote signals or barrier semaphores. Data moves between devices by JAX's collectives and lax.ppermute only.
A program may use at most 128 MiB of HBM per device.

```python
import math
import jax
import jax.numpy as jnp
from jax import lax

C = 128
H = 4
HD = 32
HC = 128
N = 1024


def marked_channels(key):
    order = jax.random.permutation(key, C).astype(jnp.int32)
    return (order[:H], order[H:2 * H])


def draw_pair(key, part):
    bias_rows, value_rows = marked_channels(key)
    key = jax.random.fold_in(key, 11)
    key_noise, key_level = jax.random.split(key)
    noise = jnp.clip(jax.random.normal(key_noise, (N, N, C), jnp.float32), -6.0, 6.0)
    level = jax.random.uniform(key_level, (N, H), jnp.float32, -2.5, 2.5)
    excess = 2.0 * jnp.maximum(-level - 0.5, 0.0)
    channel = jnp.arange(C, dtype=jnp.int32)
    on_bias = (channel[None, :] == bias_rows[:, None]).astype(jnp.float32)
    on_value = (channel[None, :] == value_rows[:, None]).astype(jnp.float32)
    column_part = jnp.sum(level[:, :, None] * on_bias[None] + excess[:, :, None] * on_value[None], axis=1)
    marked = jnp.sum(on_bias + on_value, axis=0)
    quiet = 1.0 - 0.7 * marked
    return jnp.clip(noise * quiet[None, None, :] + column_part[None], -6.0, 6.0).astype(jnp.bfloat16)


def draw_proj_weight(key, part):
    bias_rows, value_rows = marked_channels(key)
    key = jax.random.fold_in(key, 13)
    key_base, key_extra = jax.random.split(key)
    base = jax.random.normal(key_base, (2, C, 4 * HC), jnp.float32)
    base = base / math.sqrt(C)
    extra = jax.random.normal(key_extra, (4 * HC,), jnp.float32) * 2.5
    column = jnp.arange(4 * HC, dtype=jnp.int32)
    in_value = (column >= 2 * HC) & (column < 3 * HC)
    head_of = jnp.clip((column - 2 * HC) // HD, 0, H - 1)
    head_ids = jnp.arange(H, dtype=jnp.int32)
    target = jnp.sum(jnp.where(head_of[:, None] == head_ids[None, :], value_rows[None, :], 0), axis=1)
    channel = jnp.arange(C, dtype=jnp.int32)
    hit = (channel[:, None] == target[None, :]) & in_value[None, :]
    layer = jnp.arange(2, dtype=jnp.int32)
    placed = jnp.where((layer[:, None, None] == 0) & hit[None], extra[None, None, :], 0.0)
    return jnp.clip(base + placed, -8.0, 8.0).astype(jnp.bfloat16)


def draw_bias_weight(key, part):
    bias_rows, value_rows = marked_channels(key)
    key = jax.random.fold_in(key, 7)
    key_base = jax.random.fold_in(key, 0)
    channel = jnp.arange(C, dtype=jnp.int32)
    aligned = (channel[:, None] == bias_rows[None, :]).astype(jnp.float32)
    base = jax.random.normal(key_base, (2, C, H), jnp.float32)
    first = base[0] * 0.5 / math.sqrt(C) + 0.6 * aligned
    second = base[1] * 1.5 / math.sqrt(C)
    return jnp.clip(jnp.stack([first, second]), -7.0, 7.0).astype(jnp.bfloat16)


def scatter_about(rng, shape, width, limit, kind=jnp.bfloat16):
    result = width * jax.random.normal(rng, shape, jnp.float32)
    return jnp.clip(result, min=-limit, max=limit).astype(kind)


def setup_inputs(seed: int = 0) -> dict:
    seeds = jax.random.split(jax.random.key(seed), 6)
    return {
        "pair": draw_pair(jax.random.fold_in(seeds[5], 71), 0),
        "norm_gain": jnp.clip(1.0 + 0.15 * jax.random.normal(seeds[1], (2, C), jnp.float32), 0.25, 1.75),
        "proj_weight": draw_proj_weight(jax.random.fold_in(seeds[5], 71), 0),
        "out_weight": scatter_about(seeds[3], (2, HC, C), (HC // 4) ** -0.5, 1.0),
        "bias_weight": draw_bias_weight(jax.random.fold_in(seeds[5], 71), 0),
    }


def layer_norm(values, norm_scale):
    widened = values.astype(jnp.float32)
    average = lax.optimization_barrier(jnp.mean(widened, axis=-1, keepdims=True))
    centred = widened - average
    spread = lax.optimization_barrier(jnp.mean(centred * centred, axis=-1, keepdims=True))
    return (centred * lax.rsqrt(spread + 1e-05) * norm_scale).astype(jnp.bfloat16)

def project(normed, weight):
    projected = jnp.dot(normed, weight, preferred_element_type=jnp.float32)
    lead = normed.shape[:-1]
    queries = projected[..., :HC].astype(jnp.bfloat16).reshape(lead + (H, HD))
    keys_all = projected[..., HC:2 * HC].astype(jnp.bfloat16).reshape(lead + (H, HD))
    values_all = projected[..., 2 * HC:3 * HC].astype(jnp.bfloat16).reshape(lead + (H, HD))
    gates = projected[..., 3 * HC:]
    return (queries, keys_all, values_all, gates)

def attend_rows(query_block, key_block, value_block, gate_block, bias_full):
    scores = jnp.einsum('ijhc,ikhc->ijhk', query_block.astype(jnp.float32), key_block.astype(jnp.float32))
    scores = scores * HD ** (-0.5) + bias_full[None].astype(jnp.float32)
    maxima = lax.optimization_barrier(jnp.max(scores, axis=-1, keepdims=True))
    exps = jnp.exp(scores - maxima)
    weights = (exps / lax.optimization_barrier(jnp.sum(exps, axis=-1, keepdims=True))).astype(jnp.bfloat16)
    mixed = jnp.einsum('ijhk,ikhc->ijhc', weights.astype(jnp.float32), value_block.astype(jnp.float32))
    mixed = mixed.reshape(mixed.shape[:2] + (HC,))
    return (jax.nn.sigmoid(gate_block) * mixed).astype(jnp.bfloat16)

def one_pass(pair_vals, norm_scale, weight, out_w, bias_w):
    normed = layer_norm(pair_vals, norm_scale)
    queries, keys_all, values_all, gates = project(normed, weight)
    bias_vals = jnp.dot(normed, bias_w, preferred_element_type=jnp.float32).astype(jnp.bfloat16)
    bias_full = bias_vals.transpose(0, 2, 1)
    total = pair_vals.shape[0]
    inner = 4

    def per_block(block_no):
        position = (block_no * inner).astype(jnp.int32)
        return attend_rows(lax.dynamic_slice_in_dim(queries, position, inner, 0), lax.dynamic_slice_in_dim(keys_all, position, inner, 0), lax.dynamic_slice_in_dim(values_all, position, inner, 0), lax.dynamic_slice_in_dim(gates, position, inner, 0), bias_full)
    gated = lax.map(per_block, jnp.arange(total // inner, dtype=jnp.int32)).reshape(total, total, HC)
    update = jnp.dot(gated, out_w, preferred_element_type=jnp.float32)
    return (pair_vals.astype(jnp.float32) + update).astype(jnp.bfloat16)

def reference(pair, norm_gain, proj_weight, out_weight, bias_weight):
    first = one_pass(pair, norm_gain[0], proj_weight[0], out_weight[0], bias_weight[0])
    second = one_pass(first.transpose(1, 0, 2), norm_gain[1], proj_weight[1], out_weight[1], bias_weight[1])
    return second.transpose(1, 0, 2)
```

```python
import functools
import math

import jax
import jax.numpy as jnp
import numpy as np
from jax import lax
from jax.experimental import pallas as pl
from jax.experimental.pallas import tpu as pltpu
from jax.sharding import Mesh
from jax.sharding import PartitionSpec as P

BF16 = jnp.bfloat16
F32 = jnp.float32
N = 1024
C = 128
H = 4
HD = 32
CHIPS = 64
HALF = N // 2
TILE = 256
LOG2E = math.log2(math.e)
SAFE = 40.0
VMEM = 48 * 1024 * 1024
PLANE = ("x", "zh", "zl", "y")
Z = ("zh", "zl")

NT = (((1,), (1,)), ((), ()))


def dot(a, b):
    return jnp.dot(a, b, preferred_element_type=F32)


def dot_nt(a, b):
    return lax.dot_general(a, b, NT, preferred_element_type=F32)


def normalise(x, gain, ones):
    centred = x.astype(F32) - dot(x, ones[:C])
    square = centred * centred
    high = square.astype(BF16)
    low = (square - high.astype(F32)).astype(BF16)
    spread = dot(jnp.concatenate([high, low], axis=1), ones)
    return centred * lax.rsqrt(spread + 1e-5) * gain


def whole(shape):
    return pl.BlockSpec(shape, lambda *_: (0,) * len(shape))


def layer(shape, index):
    return pl.BlockSpec((1,) + shape, lambda *_: (index,) + (0,) * len(shape))


def row_spec(turned, count=1):
    if turned:
        return pl.BlockSpec((CHIPS, count, 16, C), lambda i, *_: (0, i, 0, 0))
    return pl.BlockSpec((count, N, C), lambda i, *_: (i, 0, 0))


def params():
    return pltpu.CompilerParams(vmem_limit_bytes=VMEM)


def bias_kernel(turned, index, x_ref, gain_ref, ones_ref, place_ref, out_ref, acc):
    step = pl.program_id(0)

    @pl.when(step == 0)
    def _():
        acc[...] = jnp.zeros_like(acc)

    gain = gain_ref[index : index + 1, :]
    for n in range(2):
        x = (x_ref[:, n] if turned else x_ref[n]).reshape(N, C)
        normed = normalise(x, gain, ones_ref[...]).astype(BF16)
        acc[...] += dot_nt(place_ref[0, n], normed)

    @pl.when(step == 3)
    def _():
        out_ref[...] = acc[...].astype(BF16)


def own_bias(x, gain, ones, place, turned, index):
    return pl.pallas_call(
        functools.partial(bias_kernel, turned, index),
        grid=(4,),
        in_specs=[
            row_spec(turned, 2),
            whole((2, C)),
            whole((2 * C, C)),
            pl.BlockSpec((1, 2, 32, C), lambda i: (index, i, 0, 0)),
        ],
        out_specs=whole((32, N)),
        out_shape=jax.ShapeDtypeStruct((32, N), BF16),
        scratch_shapes=[pltpu.VMEM((32, N), F32)],
        compiler_params=params(),
        cost_estimate=pl.CostEstimate(flops=2**32, bytes_accessed=2**24, transcendentals=0),
    )(x, gain, ones, place)


def project_kernel(
    index, meta_ref, x_ref, gain_ref, ones_ref, blocks_ref, w_ref, wt_ref, *refs
):
    k_ref, vt_ref, qt_ref, sigt_ref, res_ref, reach_ref, n_sc, x_sc = refs[-8:]
    step = pl.program_id(0)
    core = meta_ref[0]
    x = x_ref[...].reshape(N, C)
    normed = normalise(x, gain_ref[index : index + 1, :], ones_ref[...])
    n_sc[...] = normed.reshape(n_sc.shape)
    x_sc[...] = x.astype(F32).reshape(x_sc.shape)
    narrow = normed.astype(BF16)
    k = dot(narrow, w_ref[0, :, C : 2 * C])
    k_ref[0] = k.astype(BF16)
    vt_ref[0] = dot_nt(wt_ref[0, 2 * C : 3 * C, :], narrow).astype(BF16)
    mine = n_sc[:, pl.ds(core, 1)].reshape(HALF, C).astype(BF16)
    res_ref[0] = x_sc[:, pl.ds(core, 1)].reshape(HALF, C).astype(BF16)
    qt_ref[0] = dot_nt(wt_ref[0, :C, :], mine).astype(BF16)
    sigt_ref[0] = jax.nn.sigmoid(dot_nt(wt_ref[0, 3 * C :, :], mine))
    q = dot(mine, w_ref[0, :, :C])
    most_q = jnp.max(dot((q * q).astype(BF16), blocks_ref[...]), axis=0, keepdims=True)
    most_k = jnp.max(dot((k * k).astype(BF16), blocks_ref[...]), axis=0, keepdims=True)
    reach = jnp.broadcast_to(most_q * most_k, (8, C))

    @pl.when(step == 0)
    def _():
        reach_ref[...] = reach

    @pl.when(step > 0)
    def _():
        reach_ref[...] = jnp.maximum(reach_ref[...], reach)


def project(x, meta, gain, ones, blocks, weight, weight_t, turned, index, filled):
    first = 0 if filled is None else 8
    width = 8 if turned else 64
    split = (N // (2 * width), 2, width, C)

    def per_row(*shape):
        return pl.BlockSpec((1,) + shape, lambda i, m: (i + first,) + (0,) * len(shape))

    in_specs = [
        row_spec(turned),
        whole((2, C)),
        whole((2 * C, C)),
        whole((C, C)),
        layer((C, 4 * C), index),
        layer((4 * C, C), index),
    ]
    aliases = {}
    extra = ()
    if filled is not None:
        extra = filled
        aliases = {1 + len(in_specs) + n: n for n in range(5)}
        in_specs = in_specs + [pl.BlockSpec(memory_space=pl.ANY)] * 5
    return pl.pallas_call(
        functools.partial(project_kernel, index),
        grid_spec=pltpu.PrefetchScalarGridSpec(
            num_scalar_prefetch=1,
            grid=(8,),
            in_specs=in_specs,
            out_specs=[
                per_row(N, C),
                per_row(C, N),
                per_row(C, HALF),
                per_row(C, HALF),
                per_row(HALF, C),
                whole((8, C)),
            ],
            scratch_shapes=[pltpu.VMEM(split, F32), pltpu.VMEM(split, F32)],
        ),
        out_shape=[
            jax.ShapeDtypeStruct((16, N, C), BF16),
            jax.ShapeDtypeStruct((16, C, N), BF16),
            jax.ShapeDtypeStruct((16, C, HALF), BF16),
            jax.ShapeDtypeStruct((16, C, HALF), F32),
            jax.ShapeDtypeStruct((16, HALF, C), BF16),
            jax.ShapeDtypeStruct((8, C), F32),
        ],
        input_output_aliases=aliases,
        compiler_params=params(),
        cost_estimate=pl.CostEstimate(flops=2**33, bytes_accessed=2**25, transcendentals=2**20),
    )(meta, x, gain, ones, blocks, weight, weight_t, *extra)


def prepare_bias(meta_ref, sources, eye_ref, b_sc, bt_sc):
    y, z = meta_ref[2], meta_ref[3]
    for ref, half, start in sources:

        def body(n, _, ref=ref, half=half, start=start):
            mid = lax.div(n, 4)
            low = lax.rem(n, 4)
            at = lax.rem(z + mid + start, 4) * 4 + lax.rem(y + low, 4)
            row = pl.multiple_of(half * 128 + at * 8, 8)
            block = ref[mid, low].astype(F32)
            for h in range(H):
                b_sc[h, pl.ds(row, 8), :] = block[8 * h : 8 * h + 8]
            return 0

        lax.fori_loop(0, ref.shape[0] * 4, body, 0, unroll=2)
    for h in range(H):
        most = None
        for n in range(4):
            turned = dot_nt(eye_ref[...], b_sc[h, :, n * TILE : (n + 1) * TILE].astype(BF16))
            bt_sc[h, n * TILE : (n + 1) * TILE, :] = turned
            part = jnp.max(turned, axis=0, keepdims=True)
            most = part if most is None else jnp.maximum(most, part)
        bt_sc[h] = (bt_sc[h] - most) * LOG2E


def attend_kernel(count, *refs):
    meta_ref = refs[0]
    bias_refs = refs[1 : 1 + count]
    (
        reach_a, reach_b, k_ref, vt_ref, qa_ref, qb_ref, sa_ref, sb_ref, ra_ref, rb_ref,
        wo_ref, eye_ref, perm_ref,
    ) = refs[1 + count : 14 + count]
    out_ref, safe_sc, b_sc, bt_sc, o_sc = refs[-5:]
    step = pl.program_id(0)

    @pl.when(step == 0)
    def _():
        reach = jnp.max(jnp.maximum(reach_a[...], reach_b[...])) * (1.05 / HD)
        safe_sc[0] = (reach <= SAFE * SAFE).astype(jnp.int32)
        sources = [(bias_refs[0], 0, 0)]
        sources += [(ref, 1, 2 * n) for n, ref in enumerate(bias_refs[1:])]
        prepare_bias(meta_ref, sources, eye_ref, b_sc, bt_sc)

    def scores_of(h):
        q = jnp.concatenate([qa_ref[0], qb_ref[0]], axis=1)
        rows = [jnp.zeros((HD, TILE), BF16)] * H
        rows[h] = q[h * HD : (h + 1) * HD]
        return dot(k_ref[0], jnp.concatenate(rows, axis=0))

    def run(exact):
        mixed = []
        ahead = scores_of(0)
        for h in range(H):
            scores = ahead
            if h < H - 1:
                ahead = scores_of(h + 1)
            scores = scores * (LOG2E / math.sqrt(HD)) + bt_sc[h]
            if exact:
                scores = scores - jnp.max(scores, axis=0, keepdims=True)
            exps = jnp.exp2(scores)
            weights = (exps * (1.0 / jnp.sum(exps, axis=0, keepdims=True))).astype(BF16)
            mixed.append(dot(vt_ref[0, h * HD : (h + 1) * HD, :], weights))
        mixed = jnp.concatenate(mixed, axis=0)
        sig = jnp.concatenate([sa_ref[0], sb_ref[0]], axis=1)
        gated = dot_nt(eye_ref[...], (sig * mixed).astype(BF16)).astype(BF16)
        new = dot(gated, wo_ref[0])
        at = lax.rem(step + 8 * meta_ref[0], 16)
        o_sc[at, :128] = (ra_ref[0].astype(F32) + new[:128]).astype(BF16)
        o_sc[at, 128:] = (rb_ref[0].astype(F32) + new[128:]).astype(BF16)

    @pl.when(jnp.logical_and(step < 16, safe_sc[0] == 1))
    def _():
        run(False)

    @pl.when(jnp.logical_and(step < 16, safe_sc[0] != 1))
    def _():
        run(True)

    @pl.when(step >= 15)
    def _():
        for n in range(8):
            rows = pl.ds(pl.multiple_of((step - 15) * 128 + n * 16, 16), 16)
            piece = o_sc[:, rows, :].reshape(TILE, C)
            turned = dot(perm_ref[...], piece).astype(BF16)
            out_ref[0, 2 * n : 2 * n + 2] = turned.reshape(2, C, C)


def attend(meta, gathered, reaches, projected, wo, eye, perm, index, blocks, filled):
    k, vt, qt, sigt, res = projected

    def at(i):
        return jnp.minimum(i, 15)

    def x_of(n, m):
        return lax.rem(m[1] + n, 4)

    def lanes(n):
        return pl.BlockSpec((1, C, 128), lambda i, m: (at(i), 0, x_of(n, m)))

    def rows(n):
        return pl.BlockSpec((1, 128, C), lambda i, m: (at(i), x_of(n, m), 0))

    a, b = blocks
    in_specs = (
        [whole(g.shape) for g in gathered]
        + [whole((8, C))] * 2
        + [
            pl.BlockSpec((1, N, C), lambda i, m: (at(i), 0, 0)),
            pl.BlockSpec((1, C, N), lambda i, m: (at(i), 0, 0)),
            lanes(a),
            lanes(b),
            lanes(a),
            lanes(b),
            rows(a),
            rows(b),
            layer((C, C), index),
            whole((TILE, TILE)),
            whole((TILE, TILE)),
        ]
    )
    operands = [*gathered, *reaches, k, vt, qt, qt, sigt, sigt, res, res, wo, eye, perm]
    aliases = {}
    if filled is not None:
        aliases = {1 + len(operands): 0}
        operands.append(filled)
        in_specs.append(pl.BlockSpec(memory_space=pl.ANY))
    return pl.pallas_call(
        functools.partial(attend_kernel, len(gathered)),
        grid_spec=pltpu.PrefetchScalarGridSpec(
            num_scalar_prefetch=1,
            grid=(17,),
            in_specs=in_specs,
            out_specs=pl.BlockSpec(
                (1, 16, C, C),
                lambda i, m: (jnp.where(i < 16, x_of(a, m), x_of(b, m)), 0, 0, 0),
            ),
            scratch_shapes=[
                pltpu.SMEM((1,), jnp.int32),
                pltpu.VMEM((H, TILE, N), F32),
                pltpu.VMEM((H, N, TILE), F32),
                pltpu.VMEM((16, TILE, C), BF16),
            ],
        ),
        out_shape=jax.ShapeDtypeStruct((4, 16, C, C), BF16),
        input_output_aliases=aliases,
        compiler_params=params(),
        cost_estimate=pl.CostEstimate(flops=2**35, bytes_accessed=2**25, transcendentals=2**25),
    )(meta, *operands)


def restore_kernel(x_ref, out_ref):
    x = x_ref[...].astype(F32).reshape(8, 8, 2, 8, C)
    out_ref[0] = jnp.swapaxes(x, 1, 2).reshape(N, C).astype(BF16)


def restore(x):
    return pl.pallas_call(
        restore_kernel,
        grid=(8,),
        in_specs=[row_spec(True)],
        out_specs=row_spec(False),
        out_shape=jax.ShapeDtypeStruct((8, N, C), BF16),
        compiler_params=params(),
    )(x)


def from_ahead(value, axis, shift):
    return lax.ppermute(value, axis, [((i + shift) % 4, i) for i in range(4)])


def gather_along(block, axis):
    return jnp.stack([block] + [from_ahead(block, axis, s) for s in (1, 2, 3)])


def one_pass(x, turned, index, meta, consts, gain, weight, weight_t, wo, place):
    ones, blocks, eye, perm = consts
    other = lax.ppermute(x, "core", [(0, 1), (1, 0)])
    bias = own_bias(x, gain, ones, place, turned, index)
    plane = gather_along(gather_along(bias, "y"), Z)
    ahead = from_ahead(plane, "x", 1)
    behind = from_ahead(plane, "x", 3)
    far_low = from_ahead(ahead[:2], "x", 1)
    far_high = from_ahead(behind[2:], "x", 3)

    *projected, reach_a = project(
        x, meta, gain, ones, blocks, weight, weight_t, turned, index, None
    )
    *projected, reach_b = project(
        other, meta, gain, ones, blocks, weight, weight_t, turned, index, projected
    )
    reaches = (reach_a, reach_b)
    out = attend(
        meta, (plane, ahead), reaches, projected, wo, eye, perm, index, (0, 1), None
    )
    out = attend(
        meta, (behind, far_low, far_high), reaches, projected, wo, eye, perm, index, (3, 2), out
    )
    out = lax.all_to_all(
        out.reshape(CHIPS, C, C), PLANE, split_axis=0, concat_axis=0, tiled=True
    )
    return out.reshape(CHIPS, 8, 16, C)


def body(pair, norm_gain, proj_weight, out_weight, bias_weight):
    lane = np.arange(C)
    to = np.arange(TILE)
    source = (to % 16) * 16 + to // 16
    consts = (
        jnp.asarray(np.full((2 * C, C), 1.0 / C), BF16),
        jnp.asarray(lane[:, None] // HD == lane[None, :] // HD, BF16),
        jnp.asarray(np.eye(TILE), BF16),
        jnp.asarray(source[:, None] == to[None, :], BF16),
    )
    meta = jnp.stack(
        [lax.axis_index("core"), lax.axis_index("x"), lax.axis_index("y"), lax.axis_index(Z)]
    ).astype(jnp.int32)
    weight_t = jnp.swapaxes(proj_weight, 1, 2)
    spots = np.eye(8, dtype=np.float32)[None, :, None, :, None]
    place = jnp.swapaxes(bias_weight, 1, 2)[:, None, :, None, :] * jnp.asarray(spots, BF16)
    place = place.reshape(2, 8, 32, C)
    x = pair
    for index, turned in ((0, False), (1, True)):
        x = one_pass(
            x, turned, index, meta, consts, norm_gain, proj_weight, weight_t, out_weight, place
        )
    return restore(x)


def solution(mesh):
    fine = Mesh(mesh.devices.reshape(4, 2, 2, 2, 4), ("x", "zh", "core", "zl", "y"))
    spec = P(("x", "zh", "core", "zl", "y"), None, None)
    return jax.shard_map(
        body,
        mesh=fine,
        in_specs=(spec, P(), P(), P(), P()),
        out_specs=spec,
        check_vma=False,
    )
```

```python
import functools
import math

import jax
import jax.numpy as jnp
import numpy as np
from jax import lax
from jax.experimental import pallas as pl
from jax.experimental.pallas import tpu as pltpu
from jax.sharding import Mesh
from jax.sharding import PartitionSpec as P

BF16 = jnp.bfloat16
F32 = jnp.float32
N = 1024
C = 128
H = 4
HD = 32
CHIPS = 64
HALF = N // 2
TILE = 256
LOG2E = math.log2(math.e)
SAFE = 40.0
VMEM = 60 * 1024 * 1024
PLANE = ("x", "zh", "zl", "y")
SHEET = ("zh", "zl", "y")

NT = (((1,), (1,)), ((), ()))


def dot(a, b):
    return jnp.dot(a, b, preferred_element_type=F32)


def dot_nt(a, b):
    return lax.dot_general(a, b, NT, preferred_element_type=F32)


def normalise(x, gain, ones):
    centred = x.astype(F32) - dot(x, ones)
    spread = jnp.sum(centred * centred, axis=1, keepdims=True) * (1.0 / C)
    return centred * lax.rsqrt(spread + 1e-5) * gain


def whole(shape):
    return pl.BlockSpec(shape, lambda *_: (0,) * len(shape))


def layer(shape, index):
    return pl.BlockSpec((1,) + shape, lambda *_: (index,) + (0,) * len(shape))


def params():
    return pltpu.CompilerParams(vmem_limit_bytes=VMEM)


def pair_specs(turned):
    if turned:
        return [pl.BlockSpec((CHIPS, 2, 16, C), lambda i, m: (0, i, 0, 0))]
    shape = (2, 8, 1, 64, C)
    return [
        pl.BlockSpec(shape, lambda i, m: (i, 0, m[0], 0, 0)),
        pl.BlockSpec(shape, lambda i, m: (i, 0, 1 - m[0], 0, 0)),
    ]


def pair_rows(swapped, refs):
    for n in range(2):
        if len(refs) == 1:
            both = refs[0][:, n].astype(F32).reshape(CHIPS, 2, 8, C)
            halves = [both[:, half].reshape(HALF, C) for half in range(2)]
            if swapped:
                halves = halves[::-1]
            yield jnp.concatenate(halves, axis=0).astype(BF16)
        else:
            yield jnp.concatenate([ref[n].reshape(HALF, C) for ref in refs], axis=0)


def bias_kernel(count, index, meta_ref, *refs):
    gain_ref, ones_ref, place_ref, first_ref, second_ref, acc = refs[count:]
    step = pl.program_id(0)

    @pl.when(step == 0)
    def _():
        acc[...] = jnp.zeros_like(acc)

    gain = gain_ref[index : index + 1, :]
    for n, x in enumerate(pair_rows(False, refs[:count])):
        normed = normalise(x, gain, ones_ref[...]).astype(BF16)
        acc[...] += dot_nt(place_ref[0, n], normed)

    @pl.when(step == 3)
    def _():
        done = acc[...].astype(BF16)
        for n in range(16):
            first_ref[n] = done[:16]
            second_ref[n] = done[16:]


def own_bias(meta, pieces, gain, ones, place, turned, index):
    return pl.pallas_call(
        functools.partial(bias_kernel, len(pieces), index),
        grid_spec=pltpu.PrefetchScalarGridSpec(
            num_scalar_prefetch=1,
            grid=(4,),
            in_specs=pair_specs(turned)
            + [
                whole((2, C)),
                whole((C, C)),
                pl.BlockSpec((1, 2, 32, C), lambda i, m: (index, i, 0, 0)),
            ],
            out_specs=[whole((16, 16, N))] * 2,
            scratch_shapes=[pltpu.VMEM((32, N), F32)],
        ),
        out_shape=[jax.ShapeDtypeStruct((16, 16, N), BF16)] * 2,
        compiler_params=params(),
        cost_estimate=pl.CostEstimate(flops=2**32, bytes_accessed=2**24, transcendentals=0),
    )(meta, *pieces, gain, ones, place)


def project_kernel(count, swapped, index, meta_ref, *refs):
    gain_ref, ones_ref, blocks_ref, w_ref, wkt_ref = refs[count : count + 5]
    kt_ref, v_ref, q_ref, sig_ref, res_ref, reach_ref = refs[count + 5 :]
    step = pl.program_id(0)
    gain = gain_ref[index : index + 1, :]
    reach = None
    for n, x in enumerate(pair_rows(swapped, refs[:count])):
        normed = normalise(x, gain, ones_ref[...]).astype(BF16)
        mine = normed[:HALF]
        kt_ref[n] = dot_nt(wkt_ref[0], normed).astype(BF16)
        v_ref[n] = dot(normed, w_ref[0, :, 2 * C : 3 * C]).astype(BF16)
        q = dot(mine, w_ref[0, :, :C])
        q_ref[n] = q.astype(BF16)
        sig_ref[n] = 1.0 / (1.0 + jnp.exp(-dot(mine, w_ref[0, :, 3 * C :])))
        res_ref[n] = x[:HALF]
        k = dot(normed, w_ref[0, :, C : 2 * C])
        most_q = jnp.max(dot((q * q).astype(BF16), blocks_ref[...]), axis=0, keepdims=True)
        most_k = jnp.max(dot((k * k).astype(BF16), blocks_ref[...]), axis=0, keepdims=True)
        most = jnp.broadcast_to(most_q * most_k, (8, C))
        reach = most if reach is None else jnp.maximum(reach, most)

    @pl.when(step == 0)
    def _():
        reach_ref[...] = reach

    @pl.when(step > 0)
    def _():
        reach_ref[...] = jnp.maximum(reach_ref[...], reach)


def project(meta, pieces, gain, ones, blocks, weight, wkt, turned, index, swapped):
    def per_row(*shape):
        return pl.BlockSpec((2,) + shape, lambda i, m: (i,) + (0,) * len(shape))

    return pl.pallas_call(
        functools.partial(project_kernel, len(pieces), swapped, index),
        grid_spec=pltpu.PrefetchScalarGridSpec(
            num_scalar_prefetch=1,
            grid=(4,),
            in_specs=pair_specs(turned)
            + [
                whole((2, C)),
                whole((C, C)),
                whole((C, C)),
                layer((C, 4 * C), index),
                layer((C, C), index),
            ],
            out_specs=[
                per_row(C, N),
                per_row(N, C),
                per_row(HALF, C),
                per_row(HALF, C),
                per_row(HALF, C),
                whole((8, C)),
            ],
        ),
        out_shape=[
            jax.ShapeDtypeStruct((8, C, N), BF16),
            jax.ShapeDtypeStruct((8, N, C), BF16),
            jax.ShapeDtypeStruct((8, HALF, C), BF16),
            jax.ShapeDtypeStruct((8, HALF, C), F32),
            jax.ShapeDtypeStruct((8, HALF, C), BF16),
            jax.ShapeDtypeStruct((8, C), F32),
        ],
        compiler_params=params(),
        cost_estimate=pl.CostEstimate(flops=2**33, bytes_accessed=2**25, transcendentals=2**20),
    )(meta, *pieces, gain, ones, blocks, weight, wkt)


def prepare_bias(sources, b_sc):
    most = jnp.zeros((16, N), F32)
    for ref, head, start in sources:

        def body(n, most, ref=ref, head=head, start=start):
            row = pl.multiple_of(start + n * 8, 8)
            block = ref[n].astype(F32)
            scaled = block * LOG2E
            b_sc[pl.ds(head * TILE + row, 8), :] = scaled[:8]
            b_sc[pl.ds((head + 1) * TILE + row, 8), :] = scaled[8:]
            return jnp.maximum(most, jnp.abs(block))

        most = lax.fori_loop(0, ref.shape[0], body, most, unroll=2)
    return jnp.max(most)


def attend_kernel(count, *refs):
    bias_refs = refs[1 : 1 + 2 * count]
    own_refs, other_refs = refs[1 + 2 * count : 9 + 2 * count], refs[9 + 2 * count : 17 + 2 * count]
    reach_a, reach_b, wo_ref, mask_ref, perm_ref = refs[17 + 2 * count : 22 + 2 * count]
    out_ref, safe_sc, b_sc, o_sc = refs[-4:]
    step = pl.program_id(0)

    @pl.when(step == 0)
    def _():
        sources = []
        for pair in range(2):
            start = 0
            for ref in bias_refs[pair * count : (pair + 1) * count]:
                sources.append((ref, 2 * pair, start))
                start += ref.shape[0] * 8
        most = prepare_bias(sources, b_sc)
        reach = jnp.max(jnp.maximum(reach_a[...], reach_b[...])) * (1.05 / HD)
        safe = jnp.logical_and(reach <= SAFE * SAFE, most <= SAFE)
        safe_sc[0] = safe.astype(jnp.int32)

    def run(refs, exact):
        kt_ref, v_ref, qa_ref, qb_ref, sa_ref, sb_ref, ra_ref, rb_ref = refs
        q = jnp.concatenate([qa_ref[0], qb_ref[0]], axis=0)

        def scores_of(pair):
            heads = [q * mask_ref[h : h + 1, :] for h in (2 * pair, 2 * pair + 1)]
            return dot(jnp.concatenate(heads, axis=0), kt_ref[0])

        mixed = None
        ahead = scores_of(0)
        for pair in range(2):
            rows = slice(2 * pair * TILE, 2 * (pair + 1) * TILE)
            scores = ahead * (LOG2E / math.sqrt(HD)) + b_sc[rows, :]
            if pair == 0:
                ahead = scores_of(1)
            if exact:
                scores = scores - jnp.max(scores, axis=1, keepdims=True)
            exps = jnp.exp2(scores)
            weights = (exps * (1.0 / jnp.sum(exps, axis=1, keepdims=True))).astype(BF16)
            product = dot(weights, v_ref[0])
            for n in range(2):
                lanes = mask_ref[2 * pair + n : 2 * pair + n + 1, :].astype(F32)
                part = product[n * TILE : (n + 1) * TILE] * lanes
                mixed = part if mixed is None else mixed + part
        sig = jnp.concatenate([sa_ref[0], sb_ref[0]], axis=0)
        new = dot((sig * mixed).astype(BF16), wo_ref[0])
        o_sc[step, :128] = (ra_ref[0].astype(F32) + new[:128]).astype(BF16)
        o_sc[step, 128:] = (rb_ref[0].astype(F32) + new[128:]).astype(BF16)

    safe = safe_sc[0] == 1
    for refs, here in ((own_refs, step < 8), (other_refs, jnp.logical_and(step >= 8, step < 16))):

        @pl.when(jnp.logical_and(here, safe))
        def _(refs=refs):
            run(refs, False)

        @pl.when(jnp.logical_and(here, jnp.logical_not(safe)))
        def _(refs=refs):
            run(refs, True)

    @pl.when(step >= 15)
    def _():
        for n in range(8):
            rows = pl.ds(pl.multiple_of((step - 15) * 128 + n * 16, 16), 16)
            piece = o_sc[:, rows, :].reshape(TILE, C)
            turned = dot(perm_ref[...], piece).astype(BF16)
            out_ref[0, 2 * n : 2 * n + 2] = turned.reshape(2, C, C)


def attend(meta, gathered, projected, wo, mask, perm, index, blocks, filled):
    a, b = blocks

    def x_of(n, m):
        return lax.rem(m[1] + n, 4)

    def row_specs(first):
        def at(i):
            return jnp.clip(i - first, 0, 7)

        def rows(n):
            return pl.BlockSpec((1, 128, C), lambda i, m: (at(i), x_of(n, m), 0))

        return [
            pl.BlockSpec((1, C, N), lambda i, m: (at(i), 0, 0)),
            pl.BlockSpec((1, N, C), lambda i, m: (at(i), 0, 0)),
        ] + [rows(n) for n in (a, b) * 3]

    operands = list(gathered)
    in_specs = [whole(g.shape) for g in gathered]
    for first, (kt, v, q, sig, res, _) in zip((0, 8), projected):
        operands += [kt, v, q, q, sig, sig, res, res]
        in_specs += row_specs(first)
    operands += [projected[0][5], projected[1][5], wo, mask, perm]
    in_specs += [whole((8, C))] * 2 + [layer((C, C), index), whole((H, C)), whole((TILE, TILE))]
    aliases = {}
    if filled is not None:
        aliases = {1 + len(operands): 0}
        operands.append(filled)
        in_specs.append(pl.BlockSpec(memory_space=pl.ANY))
    return pl.pallas_call(
        functools.partial(attend_kernel, len(gathered) // 2),
        grid_spec=pltpu.PrefetchScalarGridSpec(
            num_scalar_prefetch=1,
            grid=(17,),
            in_specs=in_specs,
            out_specs=pl.BlockSpec(
                (1, 16, C, C),
                lambda i, m: (jnp.where(i < 16, x_of(a, m), x_of(b, m)), 0, 0, 0),
            ),
            scratch_shapes=[
                pltpu.SMEM((1,), jnp.int32),
                pltpu.VMEM((H * TILE, N), F32),
                pltpu.VMEM((16, TILE, C), BF16),
            ],
        ),
        out_shape=jax.ShapeDtypeStruct((4, 16, C, C), BF16),
        input_output_aliases=aliases,
        compiler_params=params(),
        cost_estimate=pl.CostEstimate(flops=2**35, bytes_accessed=2**25, transcendentals=2**25),
    )(meta, *operands)


def restore_kernel(meta_ref, x_ref, out_ref):
    for n in range(2):
        x = x_ref[:, n].astype(F32).reshape(8, 8, 2, 8, C)
        for half, core in ((0, meta_ref[0]), (1, 1 - meta_ref[0])):
            out_ref[n, :, pl.ds(core, 1)] = x[:, :, half].reshape(8, 1, 64, C).astype(BF16)


def restore(meta, x):
    out = pl.pallas_call(
        restore_kernel,
        grid_spec=pltpu.PrefetchScalarGridSpec(
            num_scalar_prefetch=1,
            grid=(4,),
            in_specs=pair_specs(True),
            out_specs=pl.BlockSpec((2, 8, 2, 64, C), lambda i, m: (i, 0, 0, 0, 0)),
        ),
        out_shape=jax.ShapeDtypeStruct((8, 8, 2, 64, C), BF16),
        compiler_params=params(),
    )(meta, x)
    return out.reshape(8, N, C)


def from_ahead(value, axis, shift):
    return lax.ppermute(value, axis, [((i + shift) % 4, i) for i in range(4)])


def exchange(value, group):
    return lax.all_to_all(value, group, split_axis=0, concat_axis=0, tiled=True)


def across(value):
    return lax.ppermute(value, "core", [(0, 1), (1, 0)])


def one_pass(own, other, turned, index, meta, consts, gain, weight, wkt, wo, place):
    ones, blocks, mask, perm = consts
    args = (gain, ones, blocks, weight, wkt, turned, index)
    low, high = own_bias(meta, own, gain, ones, place, turned, index)

    sheet_low = exchange(low, SHEET)
    sheet_low, high, *own = lax.optimization_barrier((sheet_low, high, *own))
    near_low = [from_ahead(sheet_low, "x", s) for s in (1, 3)]
    sheet_high = exchange(high, SHEET)
    own = list(project(meta, own, *args, False))

    sheet_high, own[5], *other = lax.optimization_barrier((sheet_high, own[5], *other))
    near_high = [from_ahead(sheet_high, "x", s) for s in (1, 3)]
    other = list(project(meta, other, *args, True))
    near = lax.optimization_barrier((*near_low, *near_high, other[5]))
    ahead_low, behind_low, ahead_high, behind_high, other[5] = near
    gathered = [sheet_low, ahead_low, sheet_high, ahead_high]
    far = [behind_low, from_ahead(ahead_low[:8], "x", 1), from_ahead(behind_low[8:], "x", 3)]
    far += [behind_high, from_ahead(ahead_high[:8], "x", 1), from_ahead(behind_high[8:], "x", 3)]

    out = attend(meta, gathered, (own, other), wo, mask, perm, index, (0, 1), None)
    out = attend(meta, far, (own, other), wo, mask, perm, index, (3, 2), out)
    return exchange(out.reshape(CHIPS, C, C), PLANE).reshape(CHIPS, 8, 16, C)


def body(pair, norm_gain, proj_weight, out_weight, bias_weight):
    lane = np.arange(C)
    to = np.arange(TILE)
    source = (to % 16) * 16 + to // 16
    consts = (
        jnp.asarray(np.full((C, C), 1.0 / C), BF16),
        jnp.asarray(lane[:, None] // HD == lane[None, :] // HD, BF16),
        jnp.asarray(lane[None, :] // HD == np.arange(H)[:, None], BF16),
        jnp.asarray(source[:, None] == to[None, :], BF16),
    )
    meta = jnp.stack([lax.axis_index("core"), lax.axis_index("x")]).astype(jnp.int32)
    wkt = jnp.swapaxes(proj_weight[:, :, C : 2 * C], 1, 2)
    spots = np.eye(8, dtype=np.float32)[None, :, None, :, None]
    place = jnp.swapaxes(bias_weight, 1, 2)[:, None, :, None, :] * jnp.asarray(spots, BF16)
    place = place.reshape(2, 8, 32, C)
    rest = (meta, consts, norm_gain, proj_weight, wkt, out_weight, place)

    split = (8, 8, 2, 64, C)
    own, other = pair.reshape(split), across(pair).reshape(split)
    x = one_pass([own, own], [other, other], False, 0, *rest)
    x = one_pass([x], [across(x)], True, 1, *rest)
    return restore(meta, x)


def solution(mesh):
    fine = Mesh(mesh.devices.reshape(4, 2, 2, 2, 4), ("x", "zh", "core", "zl", "y"))
    spec = P(("x", "zh", "core", "zl", "y"), None, None)
    return jax.shard_map(
        body,
        mesh=fine,
        in_specs=(spec, P(), P(), P(), P()),
        out_specs=spec,
        check_vma=False,
    )
```

```python
import functools
import math

import jax
import jax.numpy as jnp
import numpy as np
from jax import lax
from jax.experimental import pallas as pl
from jax.experimental.pallas import tpu as pltpu
from jax.sharding import Mesh
from jax.sharding import PartitionSpec as P

BF16 = jnp.bfloat16
F32 = jnp.float32
N = 1024
C = 128
H = 4
HD = 32
CHIPS = 64
HALF = N // 2
TILE = 256
LOG2E = math.log2(math.e)
SAFE = 40.0
POWER = [
    c / 2.0**15
    for c in (
        0.9999999403953552, 0.6931530833244324, 0.24015361070632935,
        0.05582631751894951, 0.008989340625703335, 0.0018775765784084797,
    )
]
DIRECT = 192
VMEM = 60 * 1024 * 1024
PLANE = ("x", "zh", "zl", "y")
SHEET = ("zh", "zl", "y")

NT = (((1,), (1,)), ((), ()))


def dot(a, b):
    return jnp.dot(a, b, preferred_element_type=F32)


def dot_nt(a, b):
    return lax.dot_general(a, b, NT, preferred_element_type=F32)


def normalise(x, gain, ones):
    centred = x.astype(F32) - dot(x, ones)
    spread = jnp.sum(centred * centred, axis=1, keepdims=True) * (1.0 / C)
    return centred * lax.rsqrt(spread + 1e-5) * gain


def whole(shape):
    return pl.BlockSpec(shape, lambda *_: (0,) * len(shape))


def layer(shape, index):
    return pl.BlockSpec((1,) + shape, lambda *_: (index,) + (0,) * len(shape))


def params():
    return pltpu.CompilerParams(vmem_limit_bytes=VMEM)


def pair_specs(turned):
    if turned:
        return [pl.BlockSpec((CHIPS, 2, 16, C), lambda i, m: (0, i, 0, 0))]
    shape = (2, 8, 1, 64, C)
    return [
        pl.BlockSpec(shape, lambda i, m: (i, 0, m[0], 0, 0)),
        pl.BlockSpec(shape, lambda i, m: (i, 0, 1 - m[0], 0, 0)),
    ]


def pair_rows(swapped, refs):
    for n in range(2):
        if len(refs) == 1:
            both = refs[0][:, n].astype(F32).reshape(CHIPS, 2, 8, C)
            halves = [both[:, half].reshape(HALF, C) for half in range(2)]
            if swapped:
                halves = halves[::-1]
            yield jnp.concatenate(halves, axis=0).astype(BF16)
        else:
            yield jnp.concatenate([ref[n].reshape(HALF, C) for ref in refs], axis=0)


def bias_kernel(count, index, meta_ref, *refs):
    gain_ref, ones_ref, place_ref, out_ref, acc = refs[count:]
    step = pl.program_id(0)

    @pl.when(step == 0)
    def _():
        acc[...] = jnp.zeros_like(acc)

    gain = gain_ref[index : index + 1, :]
    for n, x in enumerate(pair_rows(False, refs[:count])):
        normed = normalise(x, gain, ones_ref[...]).astype(BF16)
        acc[...] += dot_nt(place_ref[0, n], normed)

    @pl.when(step == 3)
    def _():
        done = acc[...].astype(BF16)
        for n in range(16):
            out_ref[n] = done


def own_bias(meta, pieces, gain, ones, place, turned, index):
    return pl.pallas_call(
        functools.partial(bias_kernel, len(pieces), index),
        grid_spec=pltpu.PrefetchScalarGridSpec(
            num_scalar_prefetch=1,
            grid=(4,),
            in_specs=pair_specs(turned)
            + [
                whole((2, C)),
                whole((C, C)),
                pl.BlockSpec((1, 2, 32, C), lambda i, m: (index, i, 0, 0)),
            ],
            out_specs=whole((16, 32, N)),
            scratch_shapes=[pltpu.VMEM((32, N), F32)],
        ),
        out_shape=jax.ShapeDtypeStruct((16, 32, N), BF16),
        compiler_params=params(),
        cost_estimate=pl.CostEstimate(flops=2**32, bytes_accessed=2**24, transcendentals=0),
    )(meta, *pieces, gain, ones, place)


def project_kernel(count, swapped, index, meta_ref, *refs):
    gain_ref, ones_ref, blocks_ref, w_ref, wt_ref = refs[count : count + 5]
    k_ref, vt_ref, qt_ref, sigt_ref, res_ref, reach_ref = refs[-6:]
    step = pl.program_id(0)
    gain = gain_ref[index : index + 1, :]
    reach = None
    for n, x in enumerate(pair_rows(swapped, refs[:count])):
        normed = normalise(x, gain, ones_ref[...]).astype(BF16)
        mine = normed[:HALF]
        k = dot(normed, w_ref[0, :, C : 2 * C])
        k_ref[n] = k.astype(BF16)
        vt_ref[n] = dot_nt(wt_ref[0, 2 * C : 3 * C, :], normed).astype(BF16)
        qt_ref[n] = dot_nt(wt_ref[0, :C, :], mine).astype(BF16)
        sigt_ref[n] = 1.0 / (1.0 + jnp.exp(-dot_nt(wt_ref[0, 3 * C :, :], mine)))
        res_ref[n] = x[:HALF]
        q = dot(mine, w_ref[0, :, :C])
        most_q = jnp.max(dot((q * q).astype(BF16), blocks_ref[...]), axis=0, keepdims=True)
        most_k = jnp.max(dot((k * k).astype(BF16), blocks_ref[...]), axis=0, keepdims=True)
        most = jnp.broadcast_to(most_q * most_k, (8, C))
        reach = most if reach is None else jnp.maximum(reach, most)

    @pl.when(step == 0)
    def _():
        reach_ref[...] = reach

    @pl.when(step > 0)
    def _():
        reach_ref[...] = jnp.maximum(reach_ref[...], reach)


def project(meta, pieces, gain, ones, blocks, weight, weight_t, turned, index, swapped, filled):
    first = 0 if filled is None else 4

    def per_row(*shape):
        return pl.BlockSpec((2,) + shape, lambda i, m: (i + first,) + (0,) * len(shape))

    in_specs = pair_specs(turned) + [
        whole((2, C)),
        whole((C, C)),
        whole((C, C)),
        layer((C, 4 * C), index),
        layer((4 * C, C), index),
    ]
    operands = [*pieces, gain, ones, blocks, weight, weight_t]
    aliases = {}
    if filled is not None:
        aliases = {1 + len(operands) + n: n for n in range(5)}
        operands += filled
        in_specs += [pl.BlockSpec(memory_space=pl.ANY)] * 5
    return pl.pallas_call(
        functools.partial(project_kernel, len(pieces), swapped, index),
        grid_spec=pltpu.PrefetchScalarGridSpec(
            num_scalar_prefetch=1,
            grid=(4,),
            in_specs=in_specs,
            out_specs=[
                per_row(N, C),
                per_row(C, N),
                per_row(C, HALF),
                per_row(C, HALF),
                per_row(HALF, C),
                whole((8, C)),
            ],
        ),
        out_shape=[
            jax.ShapeDtypeStruct((16, N, C), BF16),
            jax.ShapeDtypeStruct((16, C, N), BF16),
            jax.ShapeDtypeStruct((16, C, HALF), BF16),
            jax.ShapeDtypeStruct((16, C, HALF), F32),
            jax.ShapeDtypeStruct((16, HALF, C), BF16),
            jax.ShapeDtypeStruct((8, C), F32),
        ],
        input_output_aliases=aliases,
        compiler_params=params(),
        cost_estimate=pl.CostEstimate(flops=2**33, bytes_accessed=2**25, transcendentals=2**20),
    )(meta, *operands)


def collect_bias(sources, b_sc):
    most = jnp.zeros((32, N), F32)
    for ref, start in sources:

        def body(n, most, ref=ref, start=start):
            row = pl.multiple_of(start + n * 8, 8)
            block = ref[n].astype(F32)
            for h in range(H):
                b_sc[h, pl.ds(row, 8), :] = block[8 * h : 8 * h + 8]
            return jnp.maximum(most, jnp.abs(block))

        most = lax.fori_loop(0, ref.shape[0], body, most, unroll=2)
    return jnp.max(most)


def turn_bias(safe, eye_ref, b_sc, bt_sc):
    scale = jnp.where(safe, LOG2E / 4, LOG2E)
    shift = jnp.where(safe, 15.0, 0.0)
    for h in range(H):
        for n in range(4):
            keys = slice(n * TILE, (n + 1) * TILE)
            turned = dot_nt(eye_ref[...], b_sc[h, :, keys].astype(BF16))
            middle = n * TILE + DIRECT
            bt_sc[h, n * TILE : middle, :] = turned[:DIRECT] * LOG2E
            bt_sc[h, middle : (n + 1) * TILE, :] = turned[DIRECT:] * scale + shift


def power(u):
    whole_part = u.astype(jnp.int32)
    rest = u - whole_part.astype(F32)
    value = jnp.full_like(u, POWER[-1])
    for c in POWER[-2::-1]:
        value = value * rest + c
    value = value * lax.shift_left(jnp.ones_like(whole_part), whole_part).astype(F32)
    value = value * value
    return value * value


def attend_kernel(count, *refs):
    bias_refs = refs[1 : 1 + count]
    (
        reach_a, reach_b, k_ref, vt_ref, qa_ref, qb_ref, sa_ref, sb_ref, ra_ref, rb_ref,
        wo_ref, eye_ref, perm_ref,
    ) = refs[1 + count : 14 + count]
    out_ref, safe_sc, b_sc, bt_sc, o_sc, e0_sc, e1_sc = refs[-7:]
    e_sc = (e0_sc, e1_sc)
    step = pl.program_id(0)

    @pl.when(step == 0)
    def _():
        sources, start = [], 0
        for ref in bias_refs:
            sources.append((ref, start))
            start += ref.shape[0] * 8
        most = collect_bias(sources, b_sc)
        reach = jnp.sqrt(jnp.maximum(reach_a[...], reach_b[...]) * (1.05 / HD))
        safe = jnp.max(reach) + most <= SAFE
        safe_sc[0] = safe.astype(jnp.int32)
        turn_bias(safe, eye_ref, b_sc, bt_sc)

    def query_of(u, h):
        q = jnp.concatenate([qa_ref[u], qb_ref[u]], axis=1)
        rows = [jnp.zeros((HD, TILE), BF16)] * H
        rows[h] = q[h * HD : (h + 1) * HD]
        return jnp.concatenate(rows, axis=0)

    def finish(u, mixed):
        mixed = jnp.concatenate(mixed, axis=0)
        sig = jnp.concatenate([sa_ref[u], sb_ref[u]], axis=1)
        gated = dot_nt(eye_ref[...], (sig * mixed).astype(BF16)).astype(BF16)
        new = dot(gated, wo_ref[0])
        at = 2 * step + u
        o_sc[at, :128] = (ra_ref[u].astype(F32) + new[:128]).astype(BF16)
        o_sc[at, 128:] = (rb_ref[u].astype(F32) + new[128:]).astype(BF16)

    factor = LOG2E / math.sqrt(HD)

    def exps_of(u, h, n, query):
        first, middle = n * TILE, n * TILE + DIRECT
        scores = dot(k_ref[u, first : first + TILE, :], query)
        direct = jnp.exp2(scores[:DIRECT] * factor + bt_sc[h, first:middle, :])
        other = power(scores[DIRECT:] * (factor / 4) + bt_sc[h, middle : first + TILE, :])
        return jnp.concatenate([direct, other], axis=0)

    def run_bounded():
        tasks = [(u, h) for u in range(2) for h in range(H)]
        inverse, mixed = None, []
        for slot in range(len(tasks) + 1):
            total, product = None, None
            if slot < len(tasks):
                query = query_of(*tasks[slot])
            for n in range(4):
                rows = slice(n * TILE, (n + 1) * TILE)
                if slot < len(tasks):
                    exps = exps_of(*tasks[slot], n, query)
                    e_sc[slot % 2][rows, :] = exps
                    part = jnp.sum(exps.reshape(32, 8, TILE), axis=0)
                    total = part if total is None else total + part
                if slot > 0:
                    u, h = tasks[slot - 1]
                    weights = (e_sc[1 - slot % 2][rows, :] * inverse).astype(BF16)
                    part = dot(vt_ref[u, h * HD : (h + 1) * HD, rows], weights)
                    product = part if product is None else product + part
            if slot < len(tasks):
                inverse = 1.0 / jnp.sum(total, axis=0, keepdims=True)
            if slot > 0:
                mixed.append(product)
            if len(mixed) == H:
                finish(tasks[slot - 1][0], mixed)
                mixed = []

    def run_exact():
        for u in range(2):
            mixed = []
            for h in range(H):
                scores = dot(k_ref[u], query_of(u, h)) * factor + bt_sc[h]
                exps = jnp.exp2(scores - jnp.max(scores, axis=0, keepdims=True))
                weights = exps * (1.0 / jnp.sum(exps, axis=0, keepdims=True))
                mixed.append(dot(vt_ref[u, h * HD : (h + 1) * HD, :], weights.astype(BF16)))
            finish(u, mixed)

    @pl.when(jnp.logical_and(step < 8, safe_sc[0] == 1))
    def _():
        run_bounded()

    @pl.when(jnp.logical_and(step < 8, safe_sc[0] != 1))
    def _():
        run_exact()

    @pl.when(step >= 7)
    def _():
        for n in range(8):
            rows = pl.ds(pl.multiple_of((step - 7) * 128 + n * 16, 16), 16)
            piece = o_sc[:, rows, :].reshape(TILE, C)
            turned = dot(perm_ref[...], piece).astype(BF16)
            out_ref[0, 2 * n : 2 * n + 2] = turned.reshape(2, C, C)


def attend(meta, gathered, projected, wo, eye, perm, index, blocks, filled):
    k, vt, qt, sigt, res, *reaches = projected

    def at(i):
        return jnp.minimum(i, 7)

    def x_of(n, m):
        return lax.rem(m[1] + n, 4)

    def lanes(n):
        return pl.BlockSpec((2, C, 128), lambda i, m: (at(i), 0, x_of(n, m)))

    def rows(n):
        return pl.BlockSpec((2, 128, C), lambda i, m: (at(i), x_of(n, m), 0))

    a, b = blocks
    in_specs = (
        [whole(g.shape) for g in gathered]
        + [whole((8, C))] * 2
        + [
            pl.BlockSpec((2, N, C), lambda i, m: (at(i), 0, 0)),
            pl.BlockSpec((2, C, N), lambda i, m: (at(i), 0, 0)),
            lanes(a),
            lanes(b),
            lanes(a),
            lanes(b),
            rows(a),
            rows(b),
            layer((C, C), index),
            whole((TILE, TILE)),
            whole((TILE, TILE)),
        ]
    )
    operands = [*gathered, *reaches, k, vt, qt, qt, sigt, sigt, res, res, wo, eye, perm]
    aliases = {}
    if filled is not None:
        aliases = {1 + len(operands): 0}
        operands.append(filled)
        in_specs.append(pl.BlockSpec(memory_space=pl.ANY))
    return pl.pallas_call(
        functools.partial(attend_kernel, len(gathered)),
        grid_spec=pltpu.PrefetchScalarGridSpec(
            num_scalar_prefetch=1,
            grid=(9,),
            in_specs=in_specs,
            out_specs=pl.BlockSpec(
                (1, 16, C, C),
                lambda i, m: (jnp.where(i < 8, x_of(a, m), x_of(b, m)), 0, 0, 0),
            ),
            scratch_shapes=[
                pltpu.SMEM((1,), jnp.int32),
                pltpu.VMEM((H, TILE, N), F32),
                pltpu.VMEM((H, N, TILE), F32),
                pltpu.VMEM((16, TILE, C), BF16),
                pltpu.VMEM((N, TILE), F32),
                pltpu.VMEM((N, TILE), F32),
            ],
        ),
        out_shape=jax.ShapeDtypeStruct((4, 16, C, C), BF16),
        input_output_aliases=aliases,
        compiler_params=params(),
        cost_estimate=pl.CostEstimate(flops=2**35, bytes_accessed=2**25, transcendentals=2**25),
    )(meta, *operands)


def restore_kernel(meta_ref, x_ref, out_ref):
    for n in range(2):
        x = x_ref[:, n].astype(F32).reshape(8, 8, 2, 8, C)
        for half, core in ((0, meta_ref[0]), (1, 1 - meta_ref[0])):
            out_ref[n, :, pl.ds(core, 1)] = x[:, :, half].reshape(8, 1, 64, C).astype(BF16)


def restore(meta, x):
    out = pl.pallas_call(
        restore_kernel,
        grid_spec=pltpu.PrefetchScalarGridSpec(
            num_scalar_prefetch=1,
            grid=(4,),
            in_specs=pair_specs(True),
            out_specs=pl.BlockSpec((2, 8, 2, 64, C), lambda i, m: (i, 0, 0, 0, 0)),
        ),
        out_shape=jax.ShapeDtypeStruct((8, 8, 2, 64, C), BF16),
        compiler_params=params(),
    )(meta, x)
    return out.reshape(8, N, C)


def from_ahead(value, axis, shift):
    return lax.ppermute(value, axis, [((i + shift) % 4, i) for i in range(4)])


def exchange(value, group):
    return lax.all_to_all(value, group, split_axis=0, concat_axis=0, tiled=True)


def across(value):
    return lax.ppermute(value, "core", [(0, 1), (1, 0)])


def one_pass(own, other, turned, index, meta, consts, gain, weight, weight_t, wo, place):
    ones, blocks, eye, perm = consts
    args = (gain, ones, blocks, weight, weight_t, turned, index)
    bias = own_bias(meta, own, gain, ones, place, turned, index)
    sheet = exchange(bias, SHEET)
    ahead = from_ahead(sheet, "x", 1)
    behind = from_ahead(sheet, "x", 3)
    *filled, reach_own = project(meta, own, *args, False, None)
    *filled, reach_other = project(meta, other, *args, True, filled)
    ahead, behind, reach_other = lax.optimization_barrier((ahead, behind, reach_other))
    far_low = from_ahead(ahead[:8], "x", 1)
    far_high = from_ahead(behind[8:], "x", 3)

    rows = (*filled, reach_own, reach_other)
    out = attend(meta, (sheet, ahead), rows, wo, eye, perm, index, (0, 1), None)
    out = attend(meta, (behind, far_low, far_high), rows, wo, eye, perm, index, (3, 2), out)
    return exchange(out.reshape(CHIPS, C, C), PLANE).reshape(CHIPS, 8, 16, C)


def body(pair, norm_gain, proj_weight, out_weight, bias_weight):
    lane = np.arange(C)
    to = np.arange(TILE)
    source = (to % 16) * 16 + to // 16
    consts = (
        jnp.asarray(np.full((C, C), 1.0 / C), BF16),
        jnp.asarray(lane[:, None] // HD == lane[None, :] // HD, BF16),
        jnp.asarray(np.eye(TILE), BF16),
        jnp.asarray(source[:, None] == to[None, :], BF16),
    )
    meta = jnp.stack([lax.axis_index("core"), lax.axis_index("x")]).astype(jnp.int32)
    weight_t = jnp.swapaxes(proj_weight, 1, 2)
    spots = np.eye(8, dtype=np.float32)[None, :, None, :, None]
    place = jnp.swapaxes(bias_weight, 1, 2)[:, None, :, None, :] * jnp.asarray(spots, BF16)
    place = place.reshape(2, 8, 32, C)
    rest = (meta, consts, norm_gain, proj_weight, weight_t, out_weight, place)

    split = (8, 8, 2, 64, C)
    own, other = pair.reshape(split), across(pair).reshape(split)
    x = one_pass([own, own], [other, other], False, 0, *rest)
    x = one_pass([x], [across(x)], True, 1, *rest)
    return restore(meta, x)


def solution(mesh):
    fine = Mesh(mesh.devices.reshape(4, 2, 2, 2, 4), ("x", "zh", "core", "zl", "y"))
    spec = P(("x", "zh", "core", "zl", "y"), None, None)
    return jax.shard_map(
        body,
        mesh=fine,
        in_specs=(spec, P(), P(), P(), P()),
        out_specs=spec,
        check_vma=False,
    )
```

```python
import functools

import jax
import jax.numpy as jnp
import numpy as np
from jax import lax
from jax.experimental import pallas as pl
from jax.experimental.pallas import tpu as pltpu
from jax.sharding import Mesh
from jax.sharding import PartitionSpec as P

BF16 = jnp.bfloat16
F32 = jnp.float32
N = 1024
C = 128
H = 4
HD = 32
CHIPS = 64
HALF = N // 2
TILE = 256
SAFE = 78.0
VMEM = 60 * 1024 * 1024
PLANE = ("x", "zh", "zl", "y")
SHEET = ("zh", "zl", "y")

NT = (((1,), (1,)), ((), ()))


def dot(a, b):
    return jnp.dot(a, b, preferred_element_type=F32)


def dot_nt(a, b):
    return lax.dot_general(a, b, NT, preferred_element_type=F32)


def normalise(x, gain):
    centred = x.astype(F32) - dot(x, jnp.full((C, C), 1.0 / C, BF16))
    spread = jnp.sum(centred * centred, axis=1, keepdims=True) * (1.0 / C)
    return centred * lax.rsqrt(spread + 1e-5) * gain


def whole(shape):
    return pl.BlockSpec(shape, lambda *_: (0,) * len(shape))


def layer(shape, index):
    return pl.BlockSpec((1,) + shape, lambda *_: (index,) + (0,) * len(shape))


def params():
    return pltpu.CompilerParams(vmem_limit_bytes=VMEM)


def pair_specs(turned):
    if turned:
        return [pl.BlockSpec((CHIPS, 2, 16, C), lambda i, m: (0, i, 0, 0))]
    shape = (2, 8, 1, 64, C)
    return [
        pl.BlockSpec(shape, lambda i, m: (i, 0, m[0], 0, 0)),
        pl.BlockSpec(shape, lambda i, m: (i, 0, 1 - m[0], 0, 0)),
    ]


def pair_rows(swapped, refs):
    for n in range(2):
        if len(refs) == 1:
            both = refs[0][:, n].astype(F32).reshape(CHIPS, 2, 8, C)
            halves = [both[:, half].reshape(HALF, C) for half in range(2)]
            if swapped:
                halves = halves[::-1]
            yield jnp.concatenate(halves, axis=0).astype(BF16)
        else:
            yield jnp.concatenate([ref[n].reshape(HALF, C) for ref in refs], axis=0)


def bias_kernel(count, index, meta_ref, *refs):
    gain_ref, place_ref, out_ref, acc = refs[count:]
    step = pl.program_id(0)

    @pl.when(step == 0)
    def _():
        acc[...] = jnp.zeros_like(acc)

    gain = gain_ref[index : index + 1, :]
    for n, x in enumerate(pair_rows(False, refs[:count])):
        normed = normalise(x, gain).astype(BF16)
        acc[...] += dot_nt(place_ref[0, n], normed)

    @pl.when(step == 3)
    def _():
        done = acc[...].astype(BF16)
        for n in range(16):
            out_ref[n] = done


def own_bias(meta, pieces, gain, place, turned, index):
    return pl.pallas_call(
        functools.partial(bias_kernel, len(pieces), index),
        grid_spec=pltpu.PrefetchScalarGridSpec(
            num_scalar_prefetch=1,
            grid=(4,),
            in_specs=pair_specs(turned)
            + [
                whole((2, C)),
                pl.BlockSpec((1, 2, 32, C), lambda i, m: (index, i, 0, 0)),
            ],
            out_specs=whole((16, 32, N)),
            scratch_shapes=[pltpu.VMEM((32, N), F32)],
        ),
        out_shape=jax.ShapeDtypeStruct((16, 32, N), BF16),
        compiler_params=params(),
        cost_estimate=pl.CostEstimate(flops=2**32, bytes_accessed=2**24, transcendentals=0),
    )(meta, *pieces, gain, place)


def project_kernel(count, swapped, index, meta_ref, *refs):
    gain_ref, blocks_ref, w_ref, wt_ref = refs[count : count + 4]
    k_ref, vt_ref, qt_ref, sigt_ref, res_ref, reach_ref = refs[-6:]
    step = pl.program_id(0)
    gain = gain_ref[index : index + 1, :]
    reach = None
    for n, x in enumerate(pair_rows(swapped, refs[:count])):
        normed = normalise(x, gain).astype(BF16)
        mine = normed[:HALF]
        k = dot(normed, w_ref[0, :, C : 2 * C])
        k_ref[n] = k.astype(BF16)
        vt_ref[n] = dot_nt(wt_ref[0, 2 * C : 3 * C, :], normed).astype(BF16)
        qt_ref[n] = dot_nt(wt_ref[0, :C, :], mine).astype(BF16)
        sigt_ref[n] = 1.0 / (1.0 + jnp.exp(-dot_nt(wt_ref[0, 3 * C :, :], mine)))
        res_ref[n] = x[:HALF]
        q = dot(mine, w_ref[0, :, :C])
        most_q = jnp.max(dot((q * q).astype(BF16), blocks_ref[...]), axis=0, keepdims=True)
        most_k = jnp.max(dot((k * k).astype(BF16), blocks_ref[...]), axis=0, keepdims=True)
        most = jnp.broadcast_to(most_q * most_k, (8, C))
        reach = most if reach is None else jnp.maximum(reach, most)

    @pl.when(step == 0)
    def _():
        reach_ref[...] = reach

    @pl.when(step > 0)
    def _():
        reach_ref[...] = jnp.maximum(reach_ref[...], reach)


def project(meta, pieces, gain, blocks, weight, weight_t, turned, index, swapped, filled):
    first = 0 if filled is None else 4

    def per_row(*shape):
        return pl.BlockSpec((2,) + shape, lambda i, m: (i + first,) + (0,) * len(shape))

    in_specs = pair_specs(turned) + [
        whole((2, C)),
        whole((C, C)),
        layer((C, 4 * C), index),
        layer((4 * C, C), index),
    ]
    operands = [*pieces, gain, blocks, weight, weight_t]
    aliases = {}
    if filled is not None:
        aliases = {1 + len(operands) + n: n for n in range(5)}
        operands += filled
        in_specs += [pl.BlockSpec(memory_space=pl.ANY)] * 5
    return pl.pallas_call(
        functools.partial(project_kernel, len(pieces), swapped, index),
        grid_spec=pltpu.PrefetchScalarGridSpec(
            num_scalar_prefetch=1,
            grid=(4,),
            in_specs=in_specs,
            out_specs=[
                per_row(N, C),
                per_row(C, N),
                per_row(C, HALF),
                per_row(C, HALF),
                per_row(HALF, C),
                whole((8, C)),
            ],
        ),
        out_shape=[
            jax.ShapeDtypeStruct((16, N, C), BF16),
            jax.ShapeDtypeStruct((16, C, N), BF16),
            jax.ShapeDtypeStruct((16, C, HALF), BF16),
            jax.ShapeDtypeStruct((16, C, HALF), F32),
            jax.ShapeDtypeStruct((16, HALF, C), BF16),
            jax.ShapeDtypeStruct((8, C), F32),
        ],
        input_output_aliases=aliases,
        compiler_params=params(),
        cost_estimate=pl.CostEstimate(flops=2**33, bytes_accessed=2**25, transcendentals=2**20),
    )(meta, *operands)


def collect_bias(sources, b_sc):
    most = jnp.zeros((32, N), F32)
    for ref, start in sources:

        def body(n, most, ref=ref, start=start):
            row = pl.multiple_of(start + n * 8, 8)
            block = ref[n].astype(F32)
            for h in range(H):
                b_sc[h, pl.ds(row, 8), :] = block[8 * h : 8 * h + 8]
            return jnp.maximum(most, jnp.abs(block))

        most = lax.fori_loop(0, ref.shape[0], body, most, unroll=2)
    return jnp.max(most)


def turn_bias(eye_ref, b_sc, bt_sc):
    for h in range(H):
        for n in range(4):
            keys = slice(n * TILE, (n + 1) * TILE)
            bt_sc[h, keys, :] = dot_nt(eye_ref[...], b_sc[h, :, keys].astype(BF16))


def attend_kernel(count, *refs):
    bias_refs = refs[1 : 1 + count]
    (
        reach_a, reach_b, k_ref, vt_ref, qa_ref, qb_ref, sa_ref, sb_ref, ra_ref, rb_ref,
        wo_ref, eye_ref, perm_ref,
    ) = refs[1 + count : 14 + count]
    out_ref, safe_sc, b_sc, bt_sc, o_sc, e0_sc, e1_sc = refs[-7:]
    e_sc = (e0_sc, e1_sc)
    step = pl.program_id(0)

    @pl.when(step == 0)
    def _():
        sources, start = [], 0
        for ref in bias_refs:
            sources.append((ref, start))
            start += ref.shape[0] * 8
        most = collect_bias(sources, b_sc)
        reach = jnp.sqrt(jnp.maximum(reach_a[...], reach_b[...]) * (1.05 / HD))
        safe = jnp.max(reach) + most <= SAFE
        safe_sc[0] = safe.astype(jnp.int32)
        turn_bias(eye_ref, b_sc, bt_sc)

    def query_of(u, h):
        q = jnp.concatenate([qa_ref[u], qb_ref[u]], axis=1)
        rows = [jnp.zeros((HD, TILE), BF16)] * H
        rows[h] = q[h * HD : (h + 1) * HD]
        return jnp.concatenate(rows, axis=0)

    def finish(u, mixed):
        mixed = jnp.concatenate(mixed, axis=0)
        sig = jnp.concatenate([sa_ref[u], sb_ref[u]], axis=1)
        gated = dot_nt(eye_ref[...], (sig * mixed).astype(BF16)).astype(BF16)
        new = dot(gated, wo_ref[0])
        at = 2 * step + u
        o_sc[at, :128] = (ra_ref[u].astype(F32) + new[:128]).astype(BF16)
        o_sc[at, 128:] = (rb_ref[u].astype(F32) + new[128:]).astype(BF16)

    def scores_of(u, h, rows, query):
        return dot(k_ref[u, rows, :], query) * HD**-0.5 + bt_sc[h, rows, :]

    def run_bounded():
        tasks = [(u, h) for u in range(2) for h in range(H)]
        inverse, mixed = None, []
        for slot in range(len(tasks) + 1):
            total, product = None, None
            if slot < len(tasks):
                query = query_of(*tasks[slot])
            for n in range(4):
                rows = slice(n * TILE, (n + 1) * TILE)
                if slot < len(tasks):
                    exps = jnp.exp(scores_of(*tasks[slot], rows, query))
                    e_sc[slot % 2][rows, :] = exps
                    part = jnp.sum(exps.reshape(32, 8, TILE), axis=0)
                    total = part if total is None else total + part
                if slot > 0:
                    u, h = tasks[slot - 1]
                    weights = (e_sc[1 - slot % 2][rows, :] * inverse).astype(BF16)
                    part = dot(vt_ref[u, h * HD : (h + 1) * HD, rows], weights)
                    product = part if product is None else product + part
            if slot < len(tasks):
                inverse = 1.0 / jnp.sum(total, axis=0, keepdims=True)
            if slot > 0:
                mixed.append(product)
            if len(mixed) == H:
                finish(tasks[slot - 1][0], mixed)
                mixed = []

    def run_exact():
        for u in range(2):
            mixed = []
            for h in range(H):
                scores = scores_of(u, h, slice(0, N), query_of(u, h))
                exps = jnp.exp(scores - jnp.max(scores, axis=0, keepdims=True))
                weights = exps * (1.0 / jnp.sum(exps, axis=0, keepdims=True))
                mixed.append(dot(vt_ref[u, h * HD : (h + 1) * HD, :], weights.astype(BF16)))
            finish(u, mixed)

    @pl.when(jnp.logical_and(step < 8, safe_sc[0] == 1))
    def _():
        run_bounded()

    @pl.when(jnp.logical_and(step < 8, safe_sc[0] != 1))
    def _():
        run_exact()

    @pl.when(step >= 7)
    def _():
        for n in range(8):
            rows = pl.ds(pl.multiple_of((step - 7) * 128 + n * 16, 16), 16)
            piece = o_sc[:, rows, :].reshape(TILE, C)
            turned = dot(perm_ref[...], piece).astype(BF16)
            out_ref[0, 2 * n : 2 * n + 2] = turned.reshape(2, C, C)


def attend(meta, gathered, projected, wo, eye, perm, index, blocks, filled):
    k, vt, qt, sigt, res, *reaches = projected

    def at(i):
        return jnp.minimum(i, 7)

    def x_of(n, m):
        return lax.rem(m[1] + n, 4)

    def lanes(n):
        return pl.BlockSpec((2, C, 128), lambda i, m: (at(i), 0, x_of(n, m)))

    def rows(n):
        return pl.BlockSpec((2, 128, C), lambda i, m: (at(i), x_of(n, m), 0))

    a, b = blocks
    in_specs = (
        [whole(g.shape) for g in gathered]
        + [whole((8, C))] * 2
        + [
            pl.BlockSpec((2, N, C), lambda i, m: (at(i), 0, 0)),
            pl.BlockSpec((2, C, N), lambda i, m: (at(i), 0, 0)),
            lanes(a),
            lanes(b),
            lanes(a),
            lanes(b),
            rows(a),
            rows(b),
            layer((C, C), index),
            whole((TILE, TILE)),
            whole((TILE, TILE)),
        ]
    )
    operands = [*gathered, *reaches, k, vt, qt, qt, sigt, sigt, res, res, wo, eye, perm]
    aliases = {}
    if filled is not None:
        aliases = {1 + len(operands): 0}
        operands.append(filled)
        in_specs.append(pl.BlockSpec(memory_space=pl.ANY))
    return pl.pallas_call(
        functools.partial(attend_kernel, len(gathered)),
        grid_spec=pltpu.PrefetchScalarGridSpec(
            num_scalar_prefetch=1,
            grid=(9,),
            in_specs=in_specs,
            out_specs=pl.BlockSpec(
                (1, 16, C, C),
                lambda i, m: (jnp.where(i < 8, x_of(a, m), x_of(b, m)), 0, 0, 0),
            ),
            scratch_shapes=[
                pltpu.SMEM((1,), jnp.int32),
                pltpu.VMEM((H, TILE, N), F32),
                pltpu.VMEM((H, N, TILE), F32),
                pltpu.VMEM((16, TILE, C), BF16),
                pltpu.VMEM((N, TILE), F32),
                pltpu.VMEM((N, TILE), F32),
            ],
        ),
        out_shape=jax.ShapeDtypeStruct((4, 16, C, C), BF16),
        input_output_aliases=aliases,
        compiler_params=params(),
        cost_estimate=pl.CostEstimate(flops=2**35, bytes_accessed=2**25, transcendentals=2**25),
    )(meta, *operands)


def restore_kernel(meta_ref, x_ref, out_ref):
    for n in range(2):
        x = x_ref[:, n].astype(F32).reshape(8, 8, 2, 8, C)
        for half, core in ((0, meta_ref[0]), (1, 1 - meta_ref[0])):
            out_ref[n, :, pl.ds(core, 1)] = x[:, :, half].reshape(8, 1, 64, C).astype(BF16)


def restore(meta, x):
    out = pl.pallas_call(
        restore_kernel,
        grid_spec=pltpu.PrefetchScalarGridSpec(
            num_scalar_prefetch=1,
            grid=(4,),
            in_specs=pair_specs(True),
            out_specs=pl.BlockSpec((2, 8, 2, 64, C), lambda i, m: (i, 0, 0, 0, 0)),
        ),
        out_shape=jax.ShapeDtypeStruct((8, 8, 2, 64, C), BF16),
        compiler_params=params(),
    )(meta, x)
    return out.reshape(8, N, C)


def from_ahead(value, axis, shift):
    return lax.ppermute(value, axis, [((i + shift) % 4, i) for i in range(4)])


def exchange(value, group):
    return lax.all_to_all(value, group, split_axis=0, concat_axis=0, tiled=True)


def across(value):
    return lax.ppermute(value, "core", [(0, 1), (1, 0)])


def one_pass(own, other, turned, index, meta, consts, gain, weight, weight_t, wo, place):
    blocks, eye, perm = consts
    args = (gain, blocks, weight, weight_t, turned, index)
    bias = own_bias(meta, own, gain, place, turned, index)
    sheet = exchange(bias, SHEET)
    ahead = from_ahead(sheet, "x", 1)
    behind = from_ahead(sheet, "x", 3)
    *filled, reach_own = project(meta, own, *args, False, None)
    *filled, reach_other = project(meta, other, *args, True, filled)
    ahead, behind, reach_other = lax.optimization_barrier((ahead, behind, reach_other))
    far = from_ahead(ahead, "x", 1)

    rows = (*filled, reach_own, reach_other)
    out = attend(meta, (sheet, ahead), rows, wo, eye, perm, index, (0, 1), None)
    out = attend(meta, (behind, far), rows, wo, eye, perm, index, (3, 2), out)
    return exchange(out.reshape(CHIPS, C, C), PLANE).reshape(CHIPS, 8, 16, C)


def body(pair, norm_gain, proj_weight, out_weight, bias_weight):
    lane = np.arange(C)
    to = np.arange(TILE)
    source = (to % 16) * 16 + to // 16
    consts = (
        jnp.asarray(lane[:, None] // HD == lane[None, :] // HD, BF16),
        jnp.asarray(np.eye(TILE), BF16),
        jnp.asarray(source[:, None] == to[None, :], BF16),
    )
    meta = jnp.stack([lax.axis_index("core"), lax.axis_index("x")]).astype(jnp.int32)
    weight_t = jnp.swapaxes(proj_weight, 1, 2)
    spots = np.eye(8, dtype=np.float32)[None, :, None, :, None]
    place = jnp.swapaxes(bias_weight, 1, 2)[:, None, :, None, :] * jnp.asarray(spots, BF16)
    place = place.reshape(2, 8, 32, C)
    rest = (meta, consts, norm_gain, proj_weight, weight_t, out_weight, place)

    split = (8, 8, 2, 64, C)
    own, other = pair.reshape(split), across(pair).reshape(split)
    x = one_pass([own, own], [other, other], False, 0, *rest)
    x = one_pass([x], [across(x)], True, 1, *rest)
    return restore(meta, x)


def solution(mesh):
    fine = Mesh(mesh.devices.reshape(4, 2, 2, 2, 4), ("x", "zh", "core", "zl", "y"))
    spec = P(("x", "zh", "core", "zl", "y"), None, None)
    return jax.shard_map(
        body,
        mesh=fine,
        in_specs=(spec, P(), P(), P(), P()),
        out_specs=spec,
        check_vma=False,
    )
```

```python
import functools

import jax
import jax.numpy as jnp
import numpy as np
from jax import lax
from jax.experimental import pallas as pl
from jax.experimental.pallas import tpu as pltpu
from jax.sharding import Mesh
from jax.sharding import PartitionSpec as P

BF16 = jnp.bfloat16
F32 = jnp.float32
N = 1024
C = 128
H = 4
HD = 32
CHIPS = 64
HALF = N // 2
TILE = 256
SAFE = 78.0
VMEM = 60 * 1024 * 1024
SMALL = 24 * 1024 * 1024
ORDER = ((0, 0), (0, 1), (1, 0), (3, 1), (1, 1), (3, 0), (2, 0), (2, 1))
PLANE = ("x", "zh", "zl", "y")
SHEET = ("zh", "zl", "y")

NT = (((1,), (1,)), ((), ()))


def dot(a, b):
    return jnp.dot(a, b, preferred_element_type=F32)


def dot_nt(a, b):
    return lax.dot_general(a, b, NT, preferred_element_type=F32)


def normalise(x, gain):
    centred = x.astype(F32) - dot(x, jnp.full((C, C), 1.0 / C, BF16))
    spread = jnp.sum(centred * centred, axis=1, keepdims=True) * (1.0 / C)
    return centred * lax.rsqrt(spread + 1e-5) * gain


def whole(shape):
    return pl.BlockSpec(shape, lambda *_: (0,) * len(shape))


def layer(shape, index):
    return pl.BlockSpec((1,) + shape, lambda *_: (index,) + (0,) * len(shape))


def params(limit=VMEM):
    return pltpu.CompilerParams(vmem_limit_bytes=limit)


def group_of(meta_ref, n):
    ahead, half = ORDER[n]
    return lax.rem(meta_ref[1] + ahead, 4) * 2 + half


def pair_specs(turned):
    if turned:
        return [pl.BlockSpec((CHIPS, 2, 16, C), lambda i, m: (0, i, 0, 0))]
    shape = (2, 8, 1, 64, C)
    return [
        pl.BlockSpec(shape, lambda i, m: (i, 0, m[0], 0, 0)),
        pl.BlockSpec(shape, lambda i, m: (i, 0, 1 - m[0], 0, 0)),
    ]


def pair_rows(swapped, refs):
    for n in range(2):
        if len(refs) == 1:
            both = refs[0][:, n].astype(F32).reshape(CHIPS, 2, 8, C)
            halves = [both[:, half].reshape(HALF, C) for half in range(2)]
            if swapped:
                halves = halves[::-1]
            yield jnp.concatenate(halves, axis=0).astype(BF16)
        else:
            yield jnp.concatenate([ref[n].reshape(HALF, C) for ref in refs], axis=0)


def bias_kernel(count, index, meta_ref, *refs):
    gain_ref, place_ref, out_ref, acc = refs[count:]
    step = pl.program_id(0)

    @pl.when(step == 0)
    def _():
        acc[...] = jnp.zeros_like(acc)

    gain = gain_ref[index : index + 1, :]
    for n, x in enumerate(pair_rows(False, refs[:count])):
        normed = normalise(x, gain).astype(BF16)
        acc[...] += dot_nt(place_ref[0, n], normed)

    @pl.when(step == 3)
    def _():
        done = acc[...].astype(BF16)
        for n in range(16):
            out_ref[n] = done


def own_bias(meta, pieces, gain, place, turned, index):
    return pl.pallas_call(
        functools.partial(bias_kernel, len(pieces), index),
        grid_spec=pltpu.PrefetchScalarGridSpec(
            num_scalar_prefetch=1,
            grid=(4,),
            in_specs=pair_specs(turned)
            + [
                whole((2, C)),
                pl.BlockSpec((1, 2, 32, C), lambda i, m: (index, i, 0, 0)),
            ],
            out_specs=whole((16, 32, N)),
            scratch_shapes=[pltpu.VMEM((32, N), F32)],
        ),
        out_shape=jax.ShapeDtypeStruct((16, 32, N), BF16),
        compiler_params=params(SMALL if turned else VMEM),
        cost_estimate=pl.CostEstimate(flops=2**32, bytes_accessed=2**24, transcendentals=0),
    )(meta, *pieces, gain, place)


def project_kernel(count, swapped, index, meta_ref, *refs):
    gain_ref, blocks_ref, w_ref, wt_ref = refs[count : count + 4]
    k_ref, vt_ref, qt_ref, sigt_ref, res_ref, reach_ref, mine_sc, x_sc = refs[-8:]
    step = pl.program_id(0)
    gain = gain_ref[index : index + 1, :]
    reach = None
    for n, x in enumerate(pair_rows(swapped, refs[:count])):
        normed = normalise(x, gain).astype(BF16)
        mine_sc[n] = normed[:HALF].reshape(8, 64, C)
        x_sc[n] = x[:HALF].reshape(8, 64, C)
        groups = [group_of(meta_ref, g) for g in range(8)]
        mine = jnp.concatenate([mine_sc[n, g] for g in groups], axis=0)
        res_ref[n] = jnp.concatenate([x_sc[n, g] for g in groups], axis=0)
        k = dot(normed, w_ref[0, :, C : 2 * C])
        k_ref[n] = k.astype(BF16)
        vt_ref[n] = dot_nt(wt_ref[0, 2 * C : 3 * C, :], normed).astype(BF16)
        qt_ref[n] = dot_nt(wt_ref[0, :C, :], mine).astype(BF16)
        sigt_ref[n] = 1.0 / (1.0 + jnp.exp(-dot_nt(wt_ref[0, 3 * C :, :], mine)))
        q = dot(mine, w_ref[0, :, :C])
        most_q = jnp.max(dot((q * q).astype(BF16), blocks_ref[...]), axis=0, keepdims=True)
        most_k = jnp.max(dot((k * k).astype(BF16), blocks_ref[...]), axis=0, keepdims=True)
        most = jnp.broadcast_to(most_q * most_k, (8, C))
        reach = most if reach is None else jnp.maximum(reach, most)

    @pl.when(step == 0)
    def _():
        reach_ref[...] = reach

    @pl.when(step > 0)
    def _():
        reach_ref[...] = jnp.maximum(reach_ref[...], reach)


def project(meta, pieces, gain, blocks, weight, weight_t, turned, index, swapped, filled):
    first = 0 if filled is None else 4

    def per_row(*shape):
        return pl.BlockSpec((2,) + shape, lambda i, m: (i + first,) + (0,) * len(shape))

    in_specs = pair_specs(turned) + [
        whole((2, C)),
        whole((C, C)),
        layer((C, 4 * C), index),
        layer((4 * C, C), index),
    ]
    operands = [*pieces, gain, blocks, weight, weight_t]
    aliases = {}
    if filled is not None:
        aliases = {1 + len(operands) + n: n for n in range(5)}
        operands += filled
        in_specs += [pl.BlockSpec(memory_space=pl.ANY)] * 5
    return pl.pallas_call(
        functools.partial(project_kernel, len(pieces), swapped, index),
        grid_spec=pltpu.PrefetchScalarGridSpec(
            num_scalar_prefetch=1,
            grid=(4,),
            in_specs=in_specs,
            out_specs=[
                per_row(N, C),
                per_row(C, N),
                per_row(C, HALF),
                per_row(C, HALF),
                per_row(HALF, C),
                whole((8, C)),
            ],
            scratch_shapes=[pltpu.VMEM((2, 8, 64, C), BF16)] * 2,
        ),
        out_shape=[
            jax.ShapeDtypeStruct((16, N, C), BF16),
            jax.ShapeDtypeStruct((16, C, N), BF16),
            jax.ShapeDtypeStruct((16, C, HALF), BF16),
            jax.ShapeDtypeStruct((16, C, HALF), F32),
            jax.ShapeDtypeStruct((16, HALF, C), BF16),
            jax.ShapeDtypeStruct((8, C), F32),
        ],
        input_output_aliases=aliases,
        compiler_params=params(),
        cost_estimate=pl.CostEstimate(flops=2**33, bytes_accessed=2**25, transcendentals=2**20),
    )(meta, *operands)


def collect_bias(sources, b_sc):
    most = jnp.zeros((32, N), F32)
    for ref, start in sources:

        def body(n, most, ref=ref, start=start):
            row = pl.multiple_of(start + n * 8, 8)
            block = ref[n].astype(F32)
            for h in range(H):
                b_sc[h, pl.ds(row, 8), :] = block[8 * h : 8 * h + 8]
            return jnp.maximum(most, jnp.abs(block))

        most = lax.fori_loop(0, ref.shape[0], body, most, unroll=2)
    return jnp.max(most)


def turn_bias(eye_ref, b_sc, bt_sc):
    for h in range(H):
        for n in range(4):
            keys = slice(n * TILE, (n + 1) * TILE)
            bt_sc[h, keys, :] = dot_nt(eye_ref[...], b_sc[h, :, keys].astype(BF16))


def attend_kernel(count, *refs):
    bias_refs = refs[1 : 1 + count]
    (
        reach_a, reach_b, k_ref, vt_ref, qt_ref, sigt_ref, res_ref, wo_ref, eye_ref, perm_ref,
    ) = refs[1 + count : 11 + count]
    out_ref, safe_sc, b_sc, bt_sc, o_sc, e0_sc, e1_sc = refs[-7:]
    e_sc = (e0_sc, e1_sc)
    step = pl.program_id(0)

    @pl.when(step == 0)
    def _():
        sources, start = [], 0
        for ref in bias_refs:
            sources.append((ref, start))
            start += ref.shape[0] * 8
        most = collect_bias(sources, b_sc)
        reach = jnp.sqrt(jnp.maximum(reach_a[...], reach_b[...]) * (1.05 / HD))
        safe = jnp.max(reach) + most <= SAFE
        safe_sc[0] = safe.astype(jnp.int32)
        turn_bias(eye_ref, b_sc, bt_sc)

    def query_of(u, h):
        rows = [jnp.zeros((HD, TILE), BF16)] * H
        rows[h] = qt_ref[u, h * HD : (h + 1) * HD, :]
        return jnp.concatenate(rows, axis=0)

    def finish(u, mixed):
        mixed = jnp.concatenate(mixed, axis=0)
        gated = dot_nt(eye_ref[...], (sigt_ref[u] * mixed).astype(BF16)).astype(BF16)
        new = res_ref[u].astype(F32) + dot(gated, wo_ref[0])
        o_sc[2 * step + u] = new.astype(BF16)

    def scores_of(u, h, rows, query):
        return dot(k_ref[u, rows, :], query) * HD**-0.5 + bt_sc[h, rows, :]

    def run_bounded():
        tasks = [(u, h) for u in range(2) for h in range(H)]
        inverse, mixed = None, []
        for slot in range(len(tasks) + 1):
            total, product = None, None
            if slot < len(tasks):
                query = query_of(*tasks[slot])
            for n in range(4):
                rows = slice(n * TILE, (n + 1) * TILE)
                if slot < len(tasks):
                    exps = jnp.exp(scores_of(*tasks[slot], rows, query))
                    e_sc[slot % 2][rows, :] = exps
                    part = jnp.sum(exps.reshape(32, 8, TILE), axis=0)
                    total = part if total is None else total + part
                if slot > 0:
                    u, h = tasks[slot - 1]
                    weights = (e_sc[1 - slot % 2][rows, :] * inverse).astype(BF16)
                    part = dot(vt_ref[u, h * HD : (h + 1) * HD, rows], weights)
                    product = part if product is None else product + part
            if slot < len(tasks):
                inverse = 1.0 / jnp.sum(total, axis=0, keepdims=True)
            if slot > 0:
                mixed.append(product)
            if len(mixed) == H:
                finish(tasks[slot - 1][0], mixed)
                mixed = []

    def run_exact():
        for u in range(2):
            mixed = []
            for h in range(H):
                scores = scores_of(u, h, slice(0, N), query_of(u, h))
                exps = jnp.exp(scores - jnp.max(scores, axis=0, keepdims=True))
                weights = exps * (1.0 / jnp.sum(exps, axis=0, keepdims=True))
                mixed.append(dot(vt_ref[u, h * HD : (h + 1) * HD, :], weights.astype(BF16)))
            finish(u, mixed)

    @pl.when(jnp.logical_and(step < 8, safe_sc[0] == 1))
    def _():
        run_bounded()

    @pl.when(jnp.logical_and(step < 8, safe_sc[0] != 1))
    def _():
        run_exact()

    @pl.when(step >= 7)
    def _():
        for n in range(4):
            rows = pl.ds(pl.multiple_of((step - 7) * 64 + n * 16, 16), 16)
            piece = o_sc[:, rows, :].reshape(TILE, C)
            turned = dot(perm_ref[...], piece).astype(BF16)
            out_ref[0, 2 * n : 2 * n + 2] = turned.reshape(2, C, C)


def attend(meta, gathered, projected, wo, eye, perm, index, tile, filled):
    k, vt, qt, sigt, res, *reaches = projected

    def at(i):
        return jnp.minimum(i, 7)

    def group_at(i, m):
        groups = [group_of(m, 4 * tile + n) for n in range(4)]
        return jnp.where(
            i < 8, groups[0], jnp.where(i == 8, groups[1], jnp.where(i == 9, groups[2], groups[3]))
        )

    lanes = pl.BlockSpec((2, C, TILE), lambda i, m: (at(i), 0, tile))
    in_specs = (
        [whole(g.shape) for g in gathered]
        + [whole((8, C))] * 2
        + [
            pl.BlockSpec((2, N, C), lambda i, m: (at(i), 0, 0)),
            pl.BlockSpec((2, C, N), lambda i, m: (at(i), 0, 0)),
            lanes,
            lanes,
            pl.BlockSpec((2, TILE, C), lambda i, m: (at(i), tile, 0)),
            layer((C, C), index),
            whole((TILE, TILE)),
            whole((TILE, TILE)),
        ]
    )
    operands = [*gathered, *reaches, k, vt, qt, sigt, res, wo, eye, perm]
    aliases = {}
    if filled is not None:
        aliases = {1 + len(operands): 0}
        operands.append(filled)
        in_specs.append(pl.BlockSpec(memory_space=pl.ANY))
    return pl.pallas_call(
        functools.partial(attend_kernel, len(gathered)),
        grid_spec=pltpu.PrefetchScalarGridSpec(
            num_scalar_prefetch=1,
            grid=(11,),
            in_specs=in_specs,
            out_specs=pl.BlockSpec((1, 8, C, C), lambda i, m: (group_at(i, m), 0, 0, 0)),
            scratch_shapes=[
                pltpu.SMEM((1,), jnp.int32),
                pltpu.VMEM((H, TILE, N), F32),
                pltpu.VMEM((H, N, TILE), F32),
                pltpu.VMEM((16, TILE, C), BF16),
                pltpu.VMEM((N, TILE), F32),
                pltpu.VMEM((N, TILE), F32),
            ],
        ),
        out_shape=jax.ShapeDtypeStruct((8, 8, C, C), BF16),
        input_output_aliases=aliases,
        compiler_params=params(),
        cost_estimate=pl.CostEstimate(flops=2**35, bytes_accessed=2**25, transcendentals=2**25),
    )(meta, *operands)


def restore_kernel(meta_ref, x_ref, out_ref):
    for n in range(2):
        x = x_ref[:, n].astype(F32).reshape(8, 8, 2, 8, C)
        for half, core in ((0, meta_ref[0]), (1, 1 - meta_ref[0])):
            out_ref[n, :, pl.ds(core, 1)] = x[:, :, half].reshape(8, 1, 64, C).astype(BF16)


def restore(meta, x):
    out = pl.pallas_call(
        restore_kernel,
        grid_spec=pltpu.PrefetchScalarGridSpec(
            num_scalar_prefetch=1,
            grid=(4,),
            in_specs=pair_specs(True),
            out_specs=pl.BlockSpec((2, 8, 2, 64, C), lambda i, m: (i, 0, 0, 0, 0)),
        ),
        out_shape=jax.ShapeDtypeStruct((8, 8, 2, 64, C), BF16),
        compiler_params=params(),
    )(meta, x)
    return out.reshape(8, N, C)


def from_ahead(value, axis, shift):
    return lax.ppermute(value, axis, [((i + shift) % 4, i) for i in range(4)])


def exchange(value, group):
    return lax.all_to_all(value, group, split_axis=0, concat_axis=0, tiled=True)


def across(value):
    return lax.ppermute(value, "core", [(0, 1), (1, 0)])


def one_pass(own, other, turned, index, meta, consts, gain, weight, weight_t, wo, place):
    blocks, eye, perm = consts
    args = (gain, blocks, weight, weight_t, turned, index)
    bias = own_bias(meta, own, gain, place, turned, index)
    sheet = exchange(bias, SHEET)
    *filled, reach_own = project(meta, own, *args, False, None)
    sheet, reach_own, *other = lax.optimization_barrier((sheet, reach_own, *other))

    low, high = sheet[:8], sheet[8:]
    ahead_low, behind_high = from_ahead(low, "x", 1), from_ahead(high, "x", 3)
    *filled, reach_other = project(meta, other, *args, True, filled)
    tied = lax.optimization_barrier((low, high, ahead_low, behind_high, reach_other))
    low, high, ahead_low, behind_high, reach_other = tied
    near = (sheet, ahead_low, behind_high)
    rest = (
        from_ahead(high, "x", 1),
        from_ahead(low, "x", 3),
        from_ahead(ahead_low, "x", 1),
        from_ahead(behind_high, "x", 3),
    )

    rows = (*filled, reach_own, reach_other)
    out = attend(meta, near, rows, wo, eye, perm, index, 0, None)
    out = attend(meta, rest, rows, wo, eye, perm, index, 1, out)
    return exchange(out.reshape(CHIPS, C, C), PLANE).reshape(CHIPS, 8, 16, C)


def body(pair, norm_gain, proj_weight, out_weight, bias_weight):
    lane = np.arange(C)
    to = np.arange(TILE)
    source = (to % 16) * 16 + to // 16
    consts = (
        jnp.asarray(lane[:, None] // HD == lane[None, :] // HD, BF16),
        jnp.asarray(np.eye(TILE), BF16),
        jnp.asarray(source[:, None] == to[None, :], BF16),
    )
    meta = jnp.stack([lax.axis_index("core"), lax.axis_index("x")]).astype(jnp.int32)
    weight_t = jnp.swapaxes(proj_weight, 1, 2)
    spots = np.eye(8, dtype=np.float32)[None, :, None, :, None]
    place = jnp.swapaxes(bias_weight, 1, 2)[:, None, :, None, :] * jnp.asarray(spots, BF16)
    place = place.reshape(2, 8, 32, C)
    rest = (meta, consts, norm_gain, proj_weight, weight_t, out_weight, place)

    split = (8, 8, 2, 64, C)
    own, other = pair.reshape(split), across(pair).reshape(split)
    x = one_pass([own, own], [other, other], False, 0, *rest)
    x = one_pass([x], [across(x)], True, 1, *rest)
    return restore(meta, x)


def solution(mesh):
    fine = Mesh(mesh.devices.reshape(4, 2, 2, 2, 4), ("x", "zh", "core", "zl", "y"))
    spec = P(("x", "zh", "core", "zl", "y"), None, None)
    return jax.shard_map(
        body,
        mesh=fine,
        in_specs=(spec, P(), P(), P(), P()),
        out_specs=spec,
        check_vma=False,
    )
```

```python
import functools

import jax
import jax.numpy as jnp
import numpy as np
from jax import lax
from jax.experimental import pallas as pl
from jax.experimental.pallas import tpu as pltpu
from jax.sharding import Mesh
from jax.sharding import PartitionSpec as P

BF16 = jnp.bfloat16
F32 = jnp.float32
N = 1024
C = 128
H = 4
HD = 32
CHIPS = 64
HALF = N // 2
TILE = 256
SAFE = 78.0
VMEM = 60 * 1024 * 1024
SMALL = 24 * 1024 * 1024
ORDER = ((0, 0), (0, 1), (1, 0), (3, 1), (1, 1), (3, 0), (2, 0), (2, 1))
PLANE = ("x", "zh", "zl", "y")
SHEET = ("zh", "zl", "y")

NT = (((1,), (1,)), ((), ()))


def dot(a, b):
    return jnp.dot(a, b, preferred_element_type=F32)


def dot_nt(a, b):
    return lax.dot_general(a, b, NT, preferred_element_type=F32)


def normalise(x, gain):
    centred = x.astype(F32) - dot(x, jnp.full((C, C), 1.0 / C, BF16))
    spread = jnp.sum(centred * centred, axis=1, keepdims=True) * (1.0 / C)
    return centred * lax.rsqrt(spread + 1e-5) * gain


def whole(shape):
    return pl.BlockSpec(shape, lambda *_: (0,) * len(shape))


def layer(shape, index):
    return pl.BlockSpec((1,) + shape, lambda *_: (index,) + (0,) * len(shape))


def params(limit=VMEM):
    return pltpu.CompilerParams(vmem_limit_bytes=limit)


def group_of(meta_ref, n):
    ahead, half = ORDER[n]
    return lax.rem(meta_ref[1] + ahead, 4) * 2 + half


def pair_specs(turned):
    if turned:
        return [pl.BlockSpec((CHIPS, 2, 16, C), lambda i, m: (0, i, 0, 0))]
    shape = (2, 8, 1, 64, C)
    return [
        pl.BlockSpec(shape, lambda i, m: (i, 0, m[0], 0, 0)),
        pl.BlockSpec(shape, lambda i, m: (i, 0, 1 - m[0], 0, 0)),
    ]


def pair_rows(swapped, refs):
    for n in range(2):
        if len(refs) == 1:
            both = refs[0][:, n].astype(F32).reshape(CHIPS, 2, 8, C)
            halves = [both[:, half].reshape(HALF, C) for half in range(2)]
            if swapped:
                halves = halves[::-1]
            yield jnp.concatenate(halves, axis=0).astype(BF16)
        else:
            yield jnp.concatenate([ref[n].reshape(HALF, C) for ref in refs], axis=0)


def bias_kernel(count, index, meta_ref, *refs):
    gain_ref, heads_ref, out_ref, acc = refs[count:]
    step = pl.program_id(0)

    @pl.when(step == 0)
    def _():
        acc[...] = jnp.zeros_like(acc)

    gain = gain_ref[index : index + 1, :]
    for n, x in enumerate(pair_rows(False, refs[:count])):
        normed = normalise(x, gain).astype(BF16)
        place = lax.broadcasted_iota(jnp.int32, (32, C), 0)
        mine = jnp.where(lax.rem(place, 8) == 2 * step + n, heads_ref[0].astype(F32), 0.0)
        acc[...] += dot_nt(mine.astype(BF16), normed)

    @pl.when(step == 3)
    def _():
        done = acc[...].astype(BF16)
        for n in range(16):
            out_ref[n] = done


def own_bias(meta, pieces, gain, heads, turned, index):
    return pl.pallas_call(
        functools.partial(bias_kernel, len(pieces), index),
        grid_spec=pltpu.PrefetchScalarGridSpec(
            num_scalar_prefetch=1,
            grid=(4,),
            in_specs=pair_specs(turned)
            + [
                whole((2, C)),
                layer((32, C), index),
            ],
            out_specs=whole((16, 32, N)),
            scratch_shapes=[pltpu.VMEM((32, N), F32)],
        ),
        out_shape=jax.ShapeDtypeStruct((16, 32, N), BF16),
        compiler_params=params(SMALL if turned else VMEM),
        cost_estimate=pl.CostEstimate(flops=2**32, bytes_accessed=2**24, transcendentals=0),
    )(meta, *pieces, gain, heads)


def project_kernel(count, swapped, index, meta_ref, *refs):
    gain_ref, blocks_ref, w_ref, wt_ref = refs[count : count + 4]
    k_ref, vt_ref, qt_ref, sigt_ref, res_ref, reach_ref, mine_sc, x_sc = refs[-8:]
    step = pl.program_id(0)
    gain = gain_ref[index : index + 1, :]
    reach = None
    for n, x in enumerate(pair_rows(swapped, refs[:count])):
        normed = normalise(x, gain).astype(BF16)
        mine_sc[n] = normed[:HALF].reshape(8, 64, C)
        x_sc[n] = x[:HALF].reshape(8, 64, C)
        groups = [group_of(meta_ref, g) for g in range(8)]
        mine = jnp.concatenate([mine_sc[n, g] for g in groups], axis=0)
        res_ref[n] = jnp.concatenate([x_sc[n, g] for g in groups], axis=0)
        k = dot(normed, w_ref[0, :, C : 2 * C])
        k_ref[n] = k.astype(BF16)
        vt_ref[n] = dot_nt(wt_ref[0, 2 * C : 3 * C, :], normed).astype(BF16)
        qt_ref[n] = dot_nt(wt_ref[0, :C, :], mine).astype(BF16)
        sigt_ref[n] = 1.0 / (1.0 + jnp.exp(-dot_nt(wt_ref[0, 3 * C :, :], mine)))
        q = dot(mine, w_ref[0, :, :C])
        most_q = jnp.max(dot((q * q).astype(BF16), blocks_ref[...]), axis=0, keepdims=True)
        most_k = jnp.max(dot((k * k).astype(BF16), blocks_ref[...]), axis=0, keepdims=True)
        most = jnp.broadcast_to(most_q * most_k, (8, C))
        reach = most if reach is None else jnp.maximum(reach, most)

    @pl.when(step == 0)
    def _():
        reach_ref[...] = reach

    @pl.when(step > 0)
    def _():
        reach_ref[...] = jnp.maximum(reach_ref[...], reach)


def project(meta, pieces, gain, blocks, weight, weight_t, turned, index, swapped, filled):
    first = 0 if filled is None else 4

    def per_row(*shape):
        return pl.BlockSpec((2,) + shape, lambda i, m: (i + first,) + (0,) * len(shape))

    in_specs = pair_specs(turned) + [
        whole((2, C)),
        whole((C, C)),
        layer((C, 4 * C), index),
        layer((4 * C, C), index),
    ]
    operands = [*pieces, gain, blocks, weight, weight_t]
    aliases = {}
    if filled is not None:
        aliases = {1 + len(operands) + n: n for n in range(5)}
        operands += filled
        in_specs += [pl.BlockSpec(memory_space=pl.ANY)] * 5
    return pl.pallas_call(
        functools.partial(project_kernel, len(pieces), swapped, index),
        grid_spec=pltpu.PrefetchScalarGridSpec(
            num_scalar_prefetch=1,
            grid=(4,),
            in_specs=in_specs,
            out_specs=[
                per_row(N, C),
                per_row(C, N),
                per_row(C, HALF),
                per_row(C, HALF),
                per_row(HALF, C),
                whole((8, C)),
            ],
            scratch_shapes=[pltpu.VMEM((2, 8, 64, C), BF16)] * 2,
        ),
        out_shape=[
            jax.ShapeDtypeStruct((16, N, C), BF16),
            jax.ShapeDtypeStruct((16, C, N), BF16),
            jax.ShapeDtypeStruct((16, C, HALF), BF16),
            jax.ShapeDtypeStruct((16, C, HALF), F32),
            jax.ShapeDtypeStruct((16, HALF, C), BF16),
            jax.ShapeDtypeStruct((8, C), F32),
        ],
        input_output_aliases=aliases,
        compiler_params=params(),
        cost_estimate=pl.CostEstimate(flops=2**33, bytes_accessed=2**25, transcendentals=2**20),
    )(meta, *operands)


def collect_bias(sources, b_sc):
    most = jnp.zeros((32, N), F32)
    for ref, start in sources:

        def body(n, most, ref=ref, start=start):
            row = pl.multiple_of(start + n * 8, 8)
            block = ref[n].astype(F32)
            for h in range(H):
                b_sc[h, pl.ds(row, 8), :] = block[8 * h : 8 * h + 8]
            return jnp.maximum(most, jnp.abs(block))

        most = lax.fori_loop(0, ref.shape[0], body, most, unroll=2)
    return jnp.max(most)


def turn_bias(eye_ref, b_sc, bt_sc):
    for h in range(H):
        for n in range(8):
            keys = slice(n * C, (n + 1) * C)
            bt_sc[h, keys, :] = dot_nt(eye_ref[:C, :C], b_sc[h, :, keys].astype(BF16))


def attend_kernel(count, *refs):
    bias_refs = refs[1 : 1 + count]
    (
        reach_a, reach_b, k_ref, vt_ref, qt_ref, sigt_ref, res_ref, wo_ref, eye_ref, perm_ref,
    ) = refs[1 + count : 11 + count]
    out_ref, safe_sc, b_sc, bt_sc, o_sc, e0_sc, e1_sc = refs[-7:]
    e_sc = (e0_sc, e1_sc)
    step = pl.program_id(0)

    @pl.when(step == 0)
    def _():
        sources, start = [], 0
        for ref in bias_refs:
            sources.append((ref, start))
            start += ref.shape[0] * 8
        most = collect_bias(sources, b_sc)
        reach = jnp.sqrt(jnp.maximum(reach_a[...], reach_b[...]) * (1.05 / HD))
        safe = jnp.max(reach) + most <= SAFE
        safe_sc[0] = safe.astype(jnp.int32)
        turn_bias(eye_ref, b_sc, bt_sc)

    def query_of(u, h):
        rows = [jnp.zeros((HD, TILE), BF16)] * H
        rows[h] = qt_ref[u, h * HD : (h + 1) * HD, :]
        return jnp.concatenate(rows, axis=0)

    def finish(u, mixed):
        mixed = jnp.concatenate(mixed, axis=0)
        gated = dot_nt(eye_ref[...], (sigt_ref[u] * mixed).astype(BF16)).astype(BF16)
        new = res_ref[u].astype(F32) + dot(gated, wo_ref[0])
        o_sc[2 * step + u] = new.astype(BF16)

    def scores_of(u, h):
        return dot(k_ref[u], query_of(u, h))

    def run_bounded():
        tasks = [(u, h) for u in range(2) for h in range(H)]
        inverse, mixed = None, []
        for slot in range(len(tasks) + 1):
            total, product = None, None
            if slot < len(tasks):
                scores = scores_of(*tasks[slot])
            for n in range(4):
                rows = slice(n * TILE, (n + 1) * TILE)
                if slot < len(tasks):
                    exps = jnp.exp(scores[rows] * HD**-0.5 + bt_sc[tasks[slot][1], rows, :])
                    e_sc[slot % 2][rows, :] = exps
                    part = jnp.sum(exps.reshape(32, 8, TILE), axis=0)
                    total = part if total is None else total + part
                if slot > 0:
                    u, h = tasks[slot - 1]
                    weights = (e_sc[1 - slot % 2][rows, :] * inverse).astype(BF16)
                    part = dot(vt_ref[u, h * HD : (h + 1) * HD, rows], weights)
                    product = part if product is None else product + part
            if slot < len(tasks):
                inverse = 1.0 / jnp.sum(total, axis=0, keepdims=True)
            if slot > 0:
                mixed.append(product)
            if len(mixed) == H:
                finish(tasks[slot - 1][0], mixed)
                mixed = []

    def run_exact():
        for u in range(2):
            mixed = []
            for h in range(H):
                scores = scores_of(u, h) * HD**-0.5 + bt_sc[h]
                exps = jnp.exp(scores - jnp.max(scores, axis=0, keepdims=True))
                weights = exps * (1.0 / jnp.sum(exps, axis=0, keepdims=True))
                mixed.append(dot(vt_ref[u, h * HD : (h + 1) * HD, :], weights.astype(BF16)))
            finish(u, mixed)

    @pl.when(jnp.logical_and(step < 8, safe_sc[0] == 1))
    def _():
        run_bounded()

    @pl.when(jnp.logical_and(step < 8, safe_sc[0] != 1))
    def _():
        run_exact()

    @pl.when(step >= 7)
    def _():
        for n in range(4):
            rows = pl.ds(pl.multiple_of((step - 7) * 64 + n * 16, 16), 16)
            piece = o_sc[:, rows, :].reshape(TILE, C)
            turned = dot(perm_ref[...], piece).astype(BF16)
            out_ref[0, 2 * n : 2 * n + 2] = turned.reshape(2, C, C)


def attend(meta, gathered, projected, wo, eye, perm, index, tile, filled):
    k, vt, qt, sigt, res, *reaches = projected

    def at(i):
        return jnp.minimum(i, 7)

    def group_at(i, m):
        groups = [group_of(m, 4 * tile + n) for n in range(4)]
        return jnp.where(
            i < 8, groups[0], jnp.where(i == 8, groups[1], jnp.where(i == 9, groups[2], groups[3]))
        )

    lanes = pl.BlockSpec((2, C, TILE), lambda i, m: (at(i), 0, tile))
    in_specs = (
        [whole(g.shape) for g in gathered]
        + [whole((8, C))] * 2
        + [
            pl.BlockSpec((2, N, C), lambda i, m: (at(i), 0, 0)),
            pl.BlockSpec((2, C, N), lambda i, m: (at(i), 0, 0)),
            lanes,
            lanes,
            pl.BlockSpec((2, TILE, C), lambda i, m: (at(i), tile, 0)),
            layer((C, C), index),
            whole((TILE, TILE)),
            whole((TILE, TILE)),
        ]
    )
    operands = [*gathered, *reaches, k, vt, qt, sigt, res, wo, eye, perm]
    aliases = {}
    if filled is not None:
        aliases = {1 + len(operands): 0}
        operands.append(filled)
        in_specs.append(pl.BlockSpec(memory_space=pl.ANY))
    return pl.pallas_call(
        functools.partial(attend_kernel, len(gathered)),
        grid_spec=pltpu.PrefetchScalarGridSpec(
            num_scalar_prefetch=1,
            grid=(11,),
            in_specs=in_specs,
            out_specs=pl.BlockSpec((1, 8, C, C), lambda i, m: (group_at(i, m), 0, 0, 0)),
            scratch_shapes=[
                pltpu.SMEM((1,), jnp.int32),
                pltpu.VMEM((H, TILE, N), F32),
                pltpu.VMEM((H, N, TILE), F32),
                pltpu.VMEM((16, TILE, C), BF16),
                pltpu.VMEM((N, TILE), F32),
                pltpu.VMEM((N, TILE), F32),
            ],
        ),
        out_shape=jax.ShapeDtypeStruct((8, 8, C, C), BF16),
        input_output_aliases=aliases,
        compiler_params=params(),
        cost_estimate=pl.CostEstimate(flops=2**35, bytes_accessed=2**25, transcendentals=2**25),
    )(meta, *operands)


def restore_kernel(meta_ref, x_ref, out_ref):
    for n in range(2):
        x = x_ref[:, n].astype(F32).reshape(8, 8, 2, 8, C)
        for half, core in ((0, meta_ref[0]), (1, 1 - meta_ref[0])):
            out_ref[n, :, pl.ds(core, 1)] = x[:, :, half].reshape(8, 1, 64, C).astype(BF16)


def restore(meta, x):
    out = pl.pallas_call(
        restore_kernel,
        grid_spec=pltpu.PrefetchScalarGridSpec(
            num_scalar_prefetch=1,
            grid=(4,),
            in_specs=pair_specs(True),
            out_specs=pl.BlockSpec((2, 8, 2, 64, C), lambda i, m: (i, 0, 0, 0, 0)),
        ),
        out_shape=jax.ShapeDtypeStruct((8, 8, 2, 64, C), BF16),
        compiler_params=params(),
    )(meta, x)
    return out.reshape(8, N, C)


def from_ahead(value, axis, shift):
    return lax.ppermute(value, axis, [((i + shift) % 4, i) for i in range(4)])


def exchange(value, group):
    return lax.all_to_all(value, group, split_axis=0, concat_axis=0, tiled=True)


def across(value):
    return lax.ppermute(value, "core", [(0, 1), (1, 0)])


def one_pass(own, other, turned, index, meta, consts, gain, weight, weight_t, wo, heads):
    blocks, eye, perm = consts
    args = (gain, blocks, weight, weight_t, turned, index)
    bias = own_bias(meta, own, gain, heads, turned, index)
    sheet = exchange(bias, SHEET)
    *filled, reach_own = project(meta, own, *args, False, None)
    sheet, reach_own, *other = lax.optimization_barrier((sheet, reach_own, *other))

    low, high = sheet[:8], sheet[8:]
    ahead_low, behind_high = from_ahead(low, "x", 1), from_ahead(high, "x", 3)
    *filled, reach_other = project(meta, other, *args, True, filled)
    tied = lax.optimization_barrier((low, high, ahead_low, behind_high, reach_other))
    low, high, ahead_low, behind_high, reach_other = tied
    near = (sheet, ahead_low, behind_high)
    rest = (
        from_ahead(high, "x", 1),
        from_ahead(low, "x", 3),
        from_ahead(ahead_low, "x", 1),
        from_ahead(behind_high, "x", 3),
    )

    rows = (*filled, reach_own, reach_other)
    out = attend(meta, near, rows, wo, eye, perm, index, 0, None)
    out = attend(meta, rest, rows, wo, eye, perm, index, 1, out)
    return exchange(out.reshape(CHIPS, C, C), PLANE).reshape(CHIPS, 8, 16, C)


def body(pair, norm_gain, proj_weight, out_weight, bias_weight):
    lane = np.arange(C)
    to = np.arange(TILE)
    source = (to % 16) * 16 + to // 16
    consts = (
        jnp.asarray(lane[:, None] // HD == lane[None, :] // HD, BF16),
        jnp.asarray(np.eye(TILE), BF16),
        jnp.asarray(source[:, None] == to[None, :], BF16),
    )
    meta = jnp.stack([lax.axis_index("core"), lax.axis_index("x")]).astype(jnp.int32)
    weight_t = jnp.swapaxes(proj_weight, 1, 2)
    heads = jnp.repeat(jnp.swapaxes(bias_weight, 1, 2), 8, axis=1)
    rest = (meta, consts, norm_gain, proj_weight, weight_t, out_weight, heads)

    split = (8, 8, 2, 64, C)
    own, other = pair.reshape(split), across(pair).reshape(split)
    x = one_pass([own, own], [other, other], False, 0, *rest)
    x = one_pass([x], [across(x)], True, 1, *rest)
    return restore(meta, x)


def solution(mesh):
    fine = Mesh(mesh.devices.reshape(4, 2, 2, 2, 4), ("x", "zh", "core", "zl", "y"))
    spec = P(("x", "zh", "core", "zl", "y"), None, None)
    return jax.shard_map(
        body,
        mesh=fine,
        in_specs=(spec, P(), P(), P(), P()),
        out_specs=spec,
        check_vma=False,
    )
```

```python
import functools

import jax
import jax.numpy as jnp
import numpy as np
from jax import lax
from jax.experimental import pallas as pl
from jax.experimental.pallas import tpu as pltpu
from jax.sharding import Mesh
from jax.sharding import PartitionSpec as P

BF16 = jnp.bfloat16
F32 = jnp.float32
N = 1024
C = 128
H = 4
HD = 32
CHIPS = 64
HALF = N // 2
TILE = 256
SAFE = 78.0
VMEM = 60 * 1024 * 1024
SMALL = 24 * 1024 * 1024
ORDER = ((0, 0), (0, 1), (1, 0), (3, 1), (1, 1), (3, 0), (2, 0), (2, 1))
PLANE = ("x", "zh", "zl", "y")
SHEET = ("zh", "zl", "y")

NT = (((1,), (1,)), ((), ()))


def dot(a, b):
    return jnp.dot(a, b, preferred_element_type=F32)


def dot_nt(a, b):
    return lax.dot_general(a, b, NT, preferred_element_type=F32)


def normalise(x, gain):
    centred = x.astype(F32) - dot(x, jnp.full((C, C), 1.0 / C, BF16))
    spread = jnp.sum(centred * centred, axis=1, keepdims=True) * (1.0 / C)
    return centred * lax.rsqrt(spread + 1e-5) * gain


def whole(shape):
    return pl.BlockSpec(shape, lambda *_: (0,) * len(shape))


def layer(shape, index):
    return pl.BlockSpec((1,) + shape, lambda *_: (index,) + (0,) * len(shape))


def params(limit=VMEM):
    return pltpu.CompilerParams(vmem_limit_bytes=limit)


def group_of(meta_ref, n):
    ahead, half = ORDER[n]
    return lax.rem(meta_ref[1] + ahead, 4) * 2 + half


def pair_specs(turned):
    if turned:
        return [pl.BlockSpec((CHIPS, 2, 16, C), lambda i, m: (0, i, 0, 0))]
    shape = (2, 8, 1, 64, C)
    return [
        pl.BlockSpec(shape, lambda i, m: (i, 0, m[0], 0, 0)),
        pl.BlockSpec(shape, lambda i, m: (i, 0, 1 - m[0], 0, 0)),
    ]


def pair_rows(swapped, refs):
    for n in range(2):
        if len(refs) == 1:
            both = refs[0][:, n].astype(F32).reshape(CHIPS, 2, 8, C)
            halves = [both[:, half].reshape(HALF, C) for half in range(2)]
            if swapped:
                halves = halves[::-1]
            yield jnp.concatenate(halves, axis=0).astype(BF16)
        else:
            yield jnp.concatenate([ref[n].reshape(HALF, C) for ref in refs], axis=0)


def bias_kernel(count, index, meta_ref, *refs):
    gain_ref, heads_ref, out_ref, acc = refs[count:]
    step = pl.program_id(0)

    @pl.when(step == 0)
    def _():
        acc[...] = jnp.zeros_like(acc)

    gain = gain_ref[index : index + 1, :]
    for n, x in enumerate(pair_rows(False, refs[:count])):
        normed = normalise(x, gain).astype(BF16)
        place = lax.broadcasted_iota(jnp.int32, (32, C), 0)
        mine = jnp.where(lax.rem(place, 8) == 2 * step + n, heads_ref[0].astype(F32), 0.0)
        acc[...] += dot_nt(mine.astype(BF16), normed)

    @pl.when(step == 3)
    def _():
        done = acc[...].astype(BF16)
        for n in range(16):
            out_ref[n] = done


def own_bias(meta, pieces, gain, heads, turned, index):
    return pl.pallas_call(
        functools.partial(bias_kernel, len(pieces), index),
        grid_spec=pltpu.PrefetchScalarGridSpec(
            num_scalar_prefetch=1,
            grid=(4,),
            in_specs=pair_specs(turned)
            + [
                whole((2, C)),
                layer((32, C), index),
            ],
            out_specs=whole((16, 32, N)),
            scratch_shapes=[pltpu.VMEM((32, N), F32)],
        ),
        out_shape=jax.ShapeDtypeStruct((16, 32, N), BF16),
        compiler_params=params(SMALL if turned else VMEM),
        cost_estimate=pl.CostEstimate(flops=2**32, bytes_accessed=2**24, transcendentals=0),
    )(meta, *pieces, gain, heads)


def project_kernel(count, swapped, index, meta_ref, *refs):
    gain_ref, blocks_ref, w_ref, wt_ref = refs[count : count + 4]
    k_ref, vt_ref, qt_ref, sigt_ref, res_ref, reach_ref, mine_sc, x_sc = refs[-8:]
    step = pl.program_id(0)
    gain = gain_ref[index : index + 1, :]
    reach = None
    for n, x in enumerate(pair_rows(swapped, refs[:count])):
        normed = normalise(x, gain).astype(BF16)
        mine_sc[n] = normed[:HALF].reshape(8, 64, C)
        x_sc[n] = x[:HALF].reshape(8, 64, C)
        groups = [group_of(meta_ref, g) for g in range(8)]
        mine = jnp.concatenate([mine_sc[n, g] for g in groups], axis=0)
        res_ref[n] = jnp.concatenate([x_sc[n, g] for g in groups], axis=0)
        k = dot(normed, w_ref[0, :, C : 2 * C])
        k_ref[n] = k.astype(BF16)
        vt_ref[n] = dot_nt(wt_ref[0, 2 * C : 3 * C, :], normed).astype(BF16)
        qt_ref[n] = dot_nt(wt_ref[0, :C, :], mine).astype(BF16)
        sigt_ref[n] = 1.0 / (1.0 + jnp.exp(-dot_nt(wt_ref[0, 3 * C :, :], mine)))
        q = dot(mine, w_ref[0, :, :C])
        most_q = jnp.max(dot((q * q).astype(BF16), blocks_ref[...]), axis=0, keepdims=True)
        most_k = jnp.max(dot((k * k).astype(BF16), blocks_ref[...]), axis=0, keepdims=True)
        most = jnp.broadcast_to(most_q * most_k, (8, C))
        reach = most if reach is None else jnp.maximum(reach, most)

    @pl.when(step == 0)
    def _():
        reach_ref[...] = reach

    @pl.when(step > 0)
    def _():
        reach_ref[...] = jnp.maximum(reach_ref[...], reach)


def project(meta, pieces, gain, blocks, weight, weight_t, turned, index, swapped, filled):
    first = 0 if filled is None else 4

    def per_row(*shape):
        return pl.BlockSpec((2,) + shape, lambda i, m: (i + first,) + (0,) * len(shape))

    in_specs = pair_specs(turned) + [
        whole((2, C)),
        whole((C, C)),
        layer((C, 4 * C), index),
        layer((4 * C, C), index),
    ]
    operands = [*pieces, gain, blocks, weight, weight_t]
    aliases = {}
    if filled is not None:
        aliases = {1 + len(operands) + n: n for n in range(5)}
        operands += filled
        in_specs += [pl.BlockSpec(memory_space=pl.ANY)] * 5
    return pl.pallas_call(
        functools.partial(project_kernel, len(pieces), swapped, index),
        grid_spec=pltpu.PrefetchScalarGridSpec(
            num_scalar_prefetch=1,
            grid=(4,),
            in_specs=in_specs,
            out_specs=[
                per_row(N, C),
                per_row(C, N),
                per_row(C, HALF),
                per_row(C, HALF),
                per_row(HALF, C),
                whole((8, C)),
            ],
            scratch_shapes=[pltpu.VMEM((2, 8, 64, C), BF16)] * 2,
        ),
        out_shape=[
            jax.ShapeDtypeStruct((16, N, C), BF16),
            jax.ShapeDtypeStruct((16, C, N), BF16),
            jax.ShapeDtypeStruct((16, C, HALF), BF16),
            jax.ShapeDtypeStruct((16, C, HALF), F32),
            jax.ShapeDtypeStruct((16, HALF, C), BF16),
            jax.ShapeDtypeStruct((8, C), F32),
        ],
        input_output_aliases=aliases,
        compiler_params=params(),
        cost_estimate=pl.CostEstimate(flops=2**33, bytes_accessed=2**25, transcendentals=2**20),
    )(meta, *operands)


def collect_bias(sources, b_sc):
    most = jnp.zeros((32, N), F32)
    for ref, start in sources:

        def body(n, most, ref=ref, start=start):
            row = pl.multiple_of(start + n * 8, 8)
            block = ref[n].astype(F32)
            for h in range(H):
                b_sc[h, pl.ds(row, 8), :] = block[8 * h : 8 * h + 8]
            return jnp.maximum(most, jnp.abs(block))

        most = lax.fori_loop(0, ref.shape[0], body, most, unroll=2)
    return jnp.max(most)


def turn_bias(eye_ref, b_sc, bt_sc):
    for h in range(H):
        for n in range(8):
            keys = slice(n * C, (n + 1) * C)
            bt_sc[h, keys, :] = dot_nt(eye_ref[:C, :C], b_sc[h, :, keys].astype(BF16))


def attend_kernel(count, *refs):
    bias_refs = refs[1 : 1 + count]
    (
        reach_a, reach_b, k_ref, vt_ref, qt_ref, sigt_ref, res_ref, wo_ref, eye_ref, perm_ref,
    ) = refs[1 + count : 11 + count]
    out_ref, safe_sc, b_sc, bt_sc, o_sc, e0_sc, e1_sc = refs[-7:]
    e_sc = (e0_sc, e1_sc)
    step = pl.program_id(0)

    @pl.when(step == 0)
    def _():
        sources, start = [], 0
        for ref in bias_refs:
            sources.append((ref, start))
            start += ref.shape[0] * 8
        most = collect_bias(sources, b_sc)
        reach = jnp.sqrt(jnp.maximum(reach_a[...], reach_b[...]) * (1.05 / HD))
        safe = jnp.max(reach) + most <= SAFE
        safe_sc[0] = safe.astype(jnp.int32)
        turn_bias(eye_ref, b_sc, bt_sc)

    def query_of(u, h):
        rows = [jnp.zeros((HD, TILE), BF16)] * H
        rows[h] = qt_ref[u, h * HD : (h + 1) * HD, :]
        return jnp.concatenate(rows, axis=0)

    def finish(u, mixed):
        mixed = jnp.concatenate(mixed, axis=0)
        gated = dot_nt(eye_ref[...], (sigt_ref[u] * mixed).astype(BF16)).astype(BF16)
        new = res_ref[u].astype(F32) + dot(gated, wo_ref[0])
        o_sc[2 * step + u] = new.astype(BF16)

    def scores_of(u, h, rows, query):
        return dot(k_ref[u, rows, :], query) * HD**-0.5 + bt_sc[h, rows, :]

    def run_bounded():
        tasks = [(u, h) for u in range(2) for h in range(H)]
        inverse, mixed = None, []
        for slot in range(len(tasks) + 1):
            total, product = None, None
            if slot < len(tasks):
                query = query_of(*tasks[slot])
            for n in range(8):
                rows = slice(n * C, (n + 1) * C)
                if slot < len(tasks):
                    exps = jnp.exp(scores_of(*tasks[slot], rows, query))
                    e_sc[slot % 2][rows, :] = exps
                    part = jnp.sum(exps.reshape(16, 8, TILE), axis=0)
                    total = part if total is None else total + part
                if slot > 0:
                    u, h = tasks[slot - 1]
                    weights = (e_sc[1 - slot % 2][rows, :] * inverse).astype(BF16)
                    part = dot(vt_ref[u, h * HD : (h + 1) * HD, rows], weights)
                    product = part if product is None else product + part
            if slot < len(tasks):
                inverse = 1.0 / jnp.sum(total, axis=0, keepdims=True)
            if slot > 0:
                mixed.append(product)
            if len(mixed) == H:
                finish(tasks[slot - 1][0], mixed)
                mixed = []

    def run_exact():
        for u in range(2):
            mixed = []
            for h in range(H):
                scores = scores_of(u, h, slice(0, N), query_of(u, h))
                exps = jnp.exp(scores - jnp.max(scores, axis=0, keepdims=True))
                weights = exps * (1.0 / jnp.sum(exps, axis=0, keepdims=True))
                mixed.append(dot(vt_ref[u, h * HD : (h + 1) * HD, :], weights.astype(BF16)))
            finish(u, mixed)

    @pl.when(jnp.logical_and(step < 8, safe_sc[0] == 1))
    def _():
        run_bounded()

    @pl.when(jnp.logical_and(step < 8, safe_sc[0] != 1))
    def _():
        run_exact()

    @pl.when(step >= 7)
    def _():
        for n in range(4):
            rows = pl.ds(pl.multiple_of((step - 7) * 64 + n * 16, 16), 16)
            piece = o_sc[:, rows, :].reshape(TILE, C)
            turned = dot(perm_ref[...], piece).astype(BF16)
            out_ref[0, 2 * n : 2 * n + 2] = turned.reshape(2, C, C)


def attend(meta, gathered, projected, wo, eye, perm, index, tile, filled):
    k, vt, qt, sigt, res, *reaches = projected

    def at(i):
        return jnp.minimum(i, 7)

    def group_at(i, m):
        groups = [group_of(m, 4 * tile + n) for n in range(4)]
        return jnp.where(
            i < 8, groups[0], jnp.where(i == 8, groups[1], jnp.where(i == 9, groups[2], groups[3]))
        )

    lanes = pl.BlockSpec((2, C, TILE), lambda i, m: (at(i), 0, tile))
    in_specs = (
        [whole(g.shape) for g in gathered]
        + [whole((8, C))] * 2
        + [
            pl.BlockSpec((2, N, C), lambda i, m: (at(i), 0, 0)),
            pl.BlockSpec((2, C, N), lambda i, m: (at(i), 0, 0)),
            lanes,
            lanes,
            pl.BlockSpec((2, TILE, C), lambda i, m: (at(i), tile, 0)),
            layer((C, C), index),
            whole((TILE, TILE)),
            whole((TILE, TILE)),
        ]
    )
    operands = [*gathered, *reaches, k, vt, qt, sigt, res, wo, eye, perm]
    aliases = {}
    if filled is not None:
        aliases = {1 + len(operands): 0}
        operands.append(filled)
        in_specs.append(pl.BlockSpec(memory_space=pl.ANY))
    return pl.pallas_call(
        functools.partial(attend_kernel, len(gathered)),
        grid_spec=pltpu.PrefetchScalarGridSpec(
            num_scalar_prefetch=1,
            grid=(11,),
            in_specs=in_specs,
            out_specs=pl.BlockSpec((1, 8, C, C), lambda i, m: (group_at(i, m), 0, 0, 0)),
            scratch_shapes=[
                pltpu.SMEM((1,), jnp.int32),
                pltpu.VMEM((H, TILE, N), F32),
                pltpu.VMEM((H, N, TILE), F32),
                pltpu.VMEM((16, TILE, C), BF16),
                pltpu.VMEM((N, TILE), F32),
                pltpu.VMEM((N, TILE), F32),
            ],
        ),
        out_shape=jax.ShapeDtypeStruct((8, 8, C, C), BF16),
        input_output_aliases=aliases,
        compiler_params=params(),
        cost_estimate=pl.CostEstimate(flops=2**35, bytes_accessed=2**25, transcendentals=2**25),
    )(meta, *operands)


def restore_kernel(meta_ref, x_ref, out_ref):
    for n in range(2):
        x = x_ref[:, n].astype(F32).reshape(8, 8, 2, 8, C)
        for half, core in ((0, meta_ref[0]), (1, 1 - meta_ref[0])):
            out_ref[n, :, pl.ds(core, 1)] = x[:, :, half].reshape(8, 1, 64, C).astype(BF16)


def restore(meta, x):
    out = pl.pallas_call(
        restore_kernel,
        grid_spec=pltpu.PrefetchScalarGridSpec(
            num_scalar_prefetch=1,
            grid=(4,),
            in_specs=pair_specs(True),
            out_specs=pl.BlockSpec((2, 8, 2, 64, C), lambda i, m: (i, 0, 0, 0, 0)),
        ),
        out_shape=jax.ShapeDtypeStruct((8, 8, 2, 64, C), BF16),
        compiler_params=params(),
    )(meta, x)
    return out.reshape(8, N, C)


def from_ahead(value, axis, shift):
    return lax.ppermute(value, axis, [((i + shift) % 4, i) for i in range(4)])


def exchange(value, group):
    return lax.all_to_all(value, group, split_axis=0, concat_axis=0, tiled=True)


def across(value):
    return lax.ppermute(value, "core", [(0, 1), (1, 0)])


def one_pass(own, other, turned, index, meta, consts, gain, weight, weight_t, wo, heads):
    blocks, eye, perm = consts
    args = (gain, blocks, weight, weight_t, turned, index)
    bias = own_bias(meta, own, gain, heads, turned, index)
    sheet = exchange(bias, SHEET)
    *filled, reach_own = project(meta, own, *args, False, None)
    sheet, reach_own, *other = lax.optimization_barrier((sheet, reach_own, *other))

    low, high = sheet[:8], sheet[8:]
    ahead_low, behind_high = from_ahead(low, "x", 1), from_ahead(high, "x", 3)
    *filled, reach_other = project(meta, other, *args, True, filled)
    tied = lax.optimization_barrier((low, high, ahead_low, behind_high, reach_other))
    low, high, ahead_low, behind_high, reach_other = tied
    near = (sheet, ahead_low, behind_high)
    rest = (
        from_ahead(high, "x", 1),
        from_ahead(low, "x", 3),
        from_ahead(ahead_low, "x", 1),
        from_ahead(behind_high, "x", 3),
    )

    rows = (*filled, reach_own, reach_other)
    out = attend(meta, near, rows, wo, eye, perm, index, 0, None)
    out = attend(meta, rest, rows, wo, eye, perm, index, 1, out)
    return exchange(out.reshape(CHIPS, C, C), PLANE).reshape(CHIPS, 8, 16, C)


def body(pair, norm_gain, proj_weight, out_weight, bias_weight):
    lane = np.arange(C)
    to = np.arange(TILE)
    source = (to % 16) * 16 + to // 16
    consts = (
        jnp.asarray(lane[:, None] // HD == lane[None, :] // HD, BF16),
        jnp.asarray(np.eye(TILE), BF16),
        jnp.asarray(source[:, None] == to[None, :], BF16),
    )
    meta = jnp.stack([lax.axis_index("core"), lax.axis_index("x")]).astype(jnp.int32)
    weight_t = jnp.swapaxes(proj_weight, 1, 2)
    heads = jnp.repeat(jnp.swapaxes(bias_weight, 1, 2), 8, axis=1)
    rest = (meta, consts, norm_gain, proj_weight, weight_t, out_weight, heads)

    split = (8, 8, 2, 64, C)
    own, other = pair.reshape(split), across(pair).reshape(split)
    x = one_pass([own, own], [other, other], False, 0, *rest)
    x = one_pass([x], [across(x)], True, 1, *rest)
    return restore(meta, x)


def solution(mesh):
    fine = Mesh(mesh.devices.reshape(4, 2, 2, 2, 4), ("x", "zh", "core", "zl", "y"))
    spec = P(("x", "zh", "core", "zl", "y"), None, None)
    return jax.shard_map(
        body,
        mesh=fine,
        in_specs=(spec, P(), P(), P(), P()),
        out_specs=spec,
        check_vma=False,
    )
```
